32 devices in a mesh: ref: 8 (over z, x), win: 4 (over y, core).
Axes of the slice: x: 2, y: 2, z: 4, core: 2. Of those that a mesh axis runs over, the one named last changes fastest.
Arguments:
- queries: bfloat16 [256, 8192], P('ref', 'win'), may hold values from -1 to 1, as said below
- references: bfloat16 [8192, 8192], P('ref', 'win'), may hold values from -1 to 1, as said below
- labels: int32 [64], P('ref'), may hold values from 0 to 7, as said below
- kernel: float32 [9, 8], replicated, may hold values from 0.02 to 0.3
- class_bias: float32 [8], replicated, may hold values from -4 to 4
Outputs:
- ancestry_logprob: float32 [16, 8, 256], P('win', None, 'ref')
The draws below stay inside these ranges and needn't reach their ends.
Inputs may be any that keep to these rules, and one draw needn't show every extreme that they name: `queries`: every entry is -1 or +1. `references`: every entry is -1 or +1. Every ancestry labels at least one block.
All inputs are finite; a program needn't handle non-finite values.
Results may differ from the reference program's by a relative error of at most 0.0003.
Values may be sent and summed in bfloat16 or wider, within the bound.
No kernel may reach another device: no remote copies, remote signals or barrier semaphores. Data moves between devices by JAX's collectives and lax.ppermute only.
A program may use at most 64 MiB of HBM per device.

```python
import jax
import jax.numpy as jnp
from jax import lax

S = 512
A = 8
BLOCK = 128
TAPS = 9
NQ = 256
NR = 8192
W = 16
NBLK = 64


def genome_pair(key):
    key_refs = jax.random.fold_in(key, 11)
    key_query = jax.random.fold_in(key, 23)
    key_copy = jax.random.fold_in(key, 37)
    references = (jax.random.randint(key_refs, (NR, W * S), 0, 2) * 2 - 1).astype(jnp.float32)
    queries = (jax.random.randint(key_query, (NQ, W * S), 0, 2) * 2 - 1).astype(jnp.float32)
    copy_count = max(NQ // 8, 1)
    copy_keys = jax.random.split(key_copy, 6)
    copied_rows = jax.random.permutation(copy_keys[0], NQ)[:copy_count]
    source = jax.random.randint(copy_keys[1], (copy_count,), 0, NR // 2) * 2
    twin_rows = source + 1
    window_sites = jnp.arange(S)
    first_site = jax.random.randint(copy_keys[2], (copy_count, W, 1), 0, S)
    flip_mask = (window_sites == first_site).reshape(copy_count, W * S)
    source_rows = references[source]
    references = references.at[twin_rows].set(jnp.where(flip_mask, -source_rows, source_rows))
    levels = jnp.array([0, S // 32, S // 16], dtype=jnp.int32)
    strength = levels[jax.random.randint(copy_keys[4], (copy_count,), 0, 3)]
    noise_mask = jax.random.randint(copy_keys[5], (copy_count, W * S), 0, S) < strength[:, None]
    queries = queries.at[copied_rows].set(jnp.where(noise_mask, -source_rows, source_rows))
    return (references, queries)


def draw_queries(key, part):
    return genome_pair(key)[1].astype(jnp.bfloat16)


def draw_references(key, part):
    return genome_pair(key)[0].astype(jnp.bfloat16)


def draw_labels(key, part):
    key_label = jax.random.fold_in(key, 51)
    key_place = jax.random.fold_in(key, 53)
    labels = jax.random.randint(key_label, (NBLK,), 0, A)
    placed = jax.random.permutation(key_place, NBLK)[:A]
    return labels.at[placed].set(jnp.arange(A, dtype=jnp.int32)).astype(jnp.int32)


def noise(stream_key, extent, deviation, most, kind=jnp.bfloat16):
    values = jax.random.normal(stream_key, extent, jnp.float32) * deviation
    return jnp.minimum(jnp.maximum(values, -most), most).astype(kind)


def setup_inputs(seed: int = 0) -> dict:
    seeds = jax.random.split(jax.random.key(seed), 6)
    return {
        "queries": draw_queries(jax.random.fold_in(seeds[5], 71), 0),
        "references": draw_references(jax.random.fold_in(seeds[5], 71), 0),
        "labels": draw_labels(jax.random.fold_in(seeds[5], 71), 0),
        "kernel": jnp.clip(jax.random.uniform(seeds[3], (TAPS, A), jnp.float32, 0.02, 0.3), 0.02, 0.3),
        "class_bias": noise(seeds[4], (A,), 1.0, 4.0, jnp.float32),
    }


def reference(queries, references, labels, kernel, class_bias):
    owner_label = jnp.repeat(labels, BLOCK)
    score_scale = 256.0 / S

    def pooled_window(window):
        start_col = (window * S).astype(jnp.int32)
        query_part = lax.dynamic_slice_in_dim(queries, start_col, S, 1)
        ref_part = lax.dynamic_slice_in_dim(references, start_col, S, 1)
        scores = jnp.dot(query_part, ref_part.T, preferred_element_type=jnp.float32) * score_scale

        def ancestry_lse(ancestry):
            member = (owner_label == ancestry).astype(scores.dtype)
            return jax.nn.logsumexp(scores, axis=1, b=member[None, :])

        return lax.map(ancestry_lse, jnp.arange(A, dtype=jnp.int32))

    pooled = lax.map(pooled_window, jnp.arange(W, dtype=jnp.int32))
    centered = pooled - jnp.mean(pooled, axis=1, keepdims=True)
    half_width = TAPS // 2
    padded = jnp.pad(centered, ((half_width, half_width), (0, 0), (0, 0)))
    smoothed = jnp.zeros_like(centered)
    for offset in range(TAPS):
        smoothed = smoothed + kernel[offset][None, :, None] * padded[offset:offset + W]
    logits = smoothed + class_bias[None, :, None]
    return jax.nn.log_softmax(logits, axis=1)
```

```python
import functools

import jax
import jax.numpy as jnp
from jax import lax
from jax.experimental import pallas as pl
from jax.experimental.pallas import tpu as pltpu
from jax.sharding import PartitionSpec as P

S = 512
A = 8
BLOCK = 128
TAPS = 9
HALF = TAPS // 2

LOG2E = 1.4426950408889634
SCALE = 256.0 / S

neg_floor = -1e30


def pool_window(scores, labels_ref):
    count = scores.shape[1]
    blocks = scores.shape[0] // BLOCK
    ancestry = lax.broadcasted_iota(jnp.int32, (A, count), 0)
    peaks, totals = [], []
    for b in range(blocks):
        part = scores[b * BLOCK : (b + 1) * BLOCK]
        peak = jnp.max(part, axis=0, keepdims=True)
        totals.append(jnp.sum(jnp.exp2((part - peak) * (SCALE * LOG2E)), axis=0, keepdims=True))
        peaks.append(peak)
    members = [ancestry == labels_ref[b] for b in range(blocks)]
    group_peak = jnp.full((A, count), neg_floor, jnp.float32)
    for b in range(blocks):
        group_peak = jnp.where(members[b], jnp.maximum(group_peak, peaks[b]), group_peak)
    group_total = jnp.zeros((A, count), jnp.float32)
    for b in range(blocks):
        weight = totals[b] * jnp.exp2((peaks[b] - group_peak) * (SCALE * LOG2E))
        group_total = group_total + jnp.where(members[b], weight, 0.0)
    return jnp.where(group_total > 0, SCALE * group_peak + jnp.log(group_total), neg_floor)


def pool_body(labels_ref, refs_ref, *rest):
    query_refs, out_ref = rest[:-1], rest[-1]
    windows = refs_ref.shape[1] // S
    rows = query_refs[0].shape[0]
    pooled = []
    for window in range(windows):
        cols = slice(window * S, (window + 1) * S)
        queries = jnp.concatenate([q[:, cols] for q in query_refs], axis=0)
        scores = lax.dot_general(
            refs_ref[:, cols],
            queries,
            (((1,), (1,)), ((), ())),
            preferred_element_type=jnp.float32,
        )
        pooled.append(pool_window(scores, labels_ref))
    for j in range(len(query_refs)):
        out_ref[j] = jnp.concatenate([p[:, j * rows : (j + 1) * rows] for p in pooled], axis=1)


def pool(labels, refs, queries):
    windows = refs.shape[1] // S
    rows = queries[0].shape[0]
    count = rows * len(queries)
    return pl.pallas_call(
        pool_body,
        out_shape=jax.ShapeDtypeStruct((len(queries), A, windows * rows), jnp.float32),
        in_specs=[pl.BlockSpec(memory_space=pltpu.SMEM)]
        + [pl.BlockSpec(memory_space=pltpu.VMEM)] * (1 + len(queries)),
        out_specs=pl.BlockSpec(memory_space=pltpu.VMEM),
        cost_estimate=pl.CostEstimate(
            flops=2 * refs.size * count, bytes_accessed=2 * refs.size, transcendentals=0
        ),
        compiler_params=pltpu.CompilerParams(vmem_limit_bytes=40 << 20),
        name="pool",
    )(labels, refs, *queries)


def finish_body(win, refs, windows, place_ref, taps_ref, bias_ref, in_ref, out_ref):
    here = place_ref[0]
    rows = out_ref.shape[2]

    def centered(block):
        parts = in_ref[pl.ds(block * refs, refs)]
        highest = jnp.max(parts, axis=0)
        pooled = highest + jnp.log(jnp.sum(jnp.exp(parts - highest[None]), axis=0))
        return pooled - jnp.mean(pooled, axis=0, keepdims=True)

    before = jnp.where(here > 0, centered(jnp.maximum(here - 1, 0)), 0.0)
    after = jnp.where(here < win - 1, centered(jnp.minimum(here + 1, win - 1)), 0.0)
    padded = jnp.concatenate([before, centered(here), after], axis=1)
    width = windows * rows
    total = jnp.zeros((A, width), jnp.float32)
    for tap in range(TAPS):
        start = width + (tap - HALF) * rows
        total = total + taps_ref[:, tap : tap + 1] * padded[:, start : start + width]
    logits = total + bias_ref[...]
    shifted = logits - jnp.max(logits, axis=0, keepdims=True)
    result = shifted - jnp.log(jnp.sum(jnp.exp(shifted), axis=0, keepdims=True))
    for window in range(windows):
        out_ref[window] = result[:, window * rows : (window + 1) * rows]


def finish(received, kernel, class_bias, win, refs, windows, rows):
    place = lax.axis_index("win").astype(jnp.int32).reshape(1)
    return pl.pallas_call(
        functools.partial(finish_body, win, refs, windows),
        out_shape=jax.ShapeDtypeStruct((windows, A, rows), jnp.float32),
        in_specs=[pl.BlockSpec(memory_space=pltpu.SMEM)]
        + [pl.BlockSpec(memory_space=pltpu.VMEM)] * 3,
        out_specs=pl.BlockSpec(memory_space=pltpu.VMEM),
        name="finish",
    )(place, kernel.T, class_bias[:, None], received)


def exchange(block, offset, size):
    return lax.ppermute(block, "ref", [(i, i ^ offset) for i in range(size)])


def gather_queries(queries, size):
    blocks = {0: queries}
    far = [k for k in range(size - 2, 0, -2)]
    for k in far + [1]:
        blocks[k] = exchange(queries, k, size)
    for k in far[::-1]:
        if k == 2:
            blocks[k ^ 1] = exchange(queries, k ^ 1, size)
        else:
            blocks[k ^ 1] = exchange(blocks[k], 1, size)
    return blocks


def per_device(queries, references, labels, kernel, class_bias):
    refs, win = lax.axis_size("ref"), lax.axis_size("win")
    windows = references.shape[1] // S
    rows = queries.shape[0]
    blocks = gather_queries(queries, refs)
    early = [0, 1, 2, 3]
    late = [k for k in range(4, refs)]
    tiles = jnp.concatenate(
        [pool(labels, references, [blocks[k] for k in part]) for part in (early, late)], axis=0
    )
    owner = lax.axis_index("ref") ^ jnp.arange(refs)
    tiles = jnp.take(tiles, owner, axis=0)
    sent = jnp.broadcast_to(tiles[None], (win,) + tiles.shape).reshape((win * refs,) + tiles.shape[1:])
    received = lax.all_to_all(sent, ("win", "ref"), split_axis=0, concat_axis=0, tiled=True)
    return finish(received, kernel, class_bias, win, refs, windows, rows)


def solution(mesh):
    in_specs = (P("ref", "win"), P("ref", "win"), P("ref"), P(), P())
    out_specs = P("win", None, "ref")
    return jax.shard_map(
        per_device, mesh=mesh, in_specs=in_specs, out_specs=out_specs, check_vma=False
    )
```

```python
import functools

import jax
import jax.numpy as jnp
from jax import lax
from jax.experimental import pallas as pl
from jax.experimental.pallas import tpu as pltpu
from jax.sharding import PartitionSpec as P

S = 512
A = 8
BLOCK = 128
TAPS = 9
HALF = TAPS // 2

LOG2E = 1.4426950408889634
SCALE = 256.0 / S

neg_floor = -1e30
narrow = jnp.float8_e4m3fn
vmem = pl.BlockSpec(memory_space=pltpu.VMEM)
smem = pl.BlockSpec(memory_space=pltpu.SMEM)


def pool_window(scores, labels_ref):
    count = scores.shape[1]
    blocks = scores.shape[0] // BLOCK
    ancestry = lax.broadcasted_iota(jnp.int32, (A, count), 0)
    peaks, totals = [], []
    for b in range(blocks):
        part = scores[b * BLOCK : (b + 1) * BLOCK]
        peak = jnp.max(part, axis=0, keepdims=True)
        totals.append(jnp.sum(jnp.exp2((part - peak) * (SCALE * LOG2E)), axis=0, keepdims=True))
        peaks.append(peak)
    members = [ancestry == labels_ref[b] for b in range(blocks)]
    group_peak = jnp.full((A, count), neg_floor, jnp.float32)
    for b in range(blocks):
        group_peak = jnp.where(members[b], jnp.maximum(group_peak, peaks[b]), group_peak)
    group_total = jnp.zeros((A, count), jnp.float32)
    for b in range(blocks):
        weight = totals[b] * jnp.exp2((peaks[b] - group_peak) * (SCALE * LOG2E))
        group_total = group_total + jnp.where(members[b], weight, 0.0)
    return jnp.where(group_total > 0, SCALE * group_peak + jnp.log(group_total), neg_floor)


def stage_body(refs_ref, queries_ref, out_ref, mine_ref, chunks, sems):
    count, step = chunks.shape[0], chunks.shape[1]
    copies = [
        pltpu.make_async_copy(refs_ref.at[pl.ds(c * step, step)], chunks.at[c], sems.at[c])
        for c in range(count)
    ]
    copies.append(pltpu.make_async_copy(queries_ref, mine_ref, sems.at[count]))
    for copy in copies:
        copy.start()
    for c in range(count):
        copies[c].wait()
        out_ref[c * step : (c + 1) * step] = chunks[c].astype(narrow)
    copies[count].wait()


def stage(references, queries):
    step = 128
    count = references.shape[0] // step
    return pl.pallas_call(
        stage_body,
        out_shape=(
            pltpu.VMEM(references.shape, narrow),
            pltpu.VMEM(queries.shape, queries.dtype),
        ),
        in_specs=[pl.BlockSpec(memory_space=pl.ANY)] * 2,
        out_specs=(vmem, vmem),
        scratch_shapes=[
            pltpu.VMEM((count, step, references.shape[1]), references.dtype),
            pltpu.SemaphoreType.DMA((count + 1,)),
        ],
        cost_estimate=pl.CostEstimate(
            flops=references.size, bytes_accessed=3 * references.size, transcendentals=0
        ),
        compiler_params=pltpu.CompilerParams(vmem_limit_bytes=40 << 20),
        name="stage",
    )(*(pltpu.with_memory_space_constraint(x, pltpu.HBM) for x in (references, queries)))


def pool_tiles(labels_ref, refs_ref, query_refs):
    windows = refs_ref.shape[1] // S
    rows = query_refs[0].shape[0]
    pooled = []
    for window in range(windows):
        cols = slice(window * S, (window + 1) * S)
        queries = jnp.concatenate([q[:, cols] for q in query_refs], axis=0)
        scores = lax.dot_general(
            refs_ref[:, cols],
            queries.astype(narrow),
            (((1,), (1,)), ((), ())),
            preferred_element_type=jnp.float32,
        )
        pooled.append(pool_window(scores, labels_ref))
    return [
        jnp.concatenate([p[:, j * rows : (j + 1) * rows] for p in pooled], axis=1)
        for j in range(len(query_refs))
    ]


def pool_body(labels_ref, refs_ref, *rest):
    out_ref = rest[-1]
    for j, tile in enumerate(pool_tiles(labels_ref, refs_ref, rest[:-1])):
        out_ref[j] = tile


def last_body(late, groups, here_ref, labels_ref, refs_ref, *rest):
    out_ref = rest[-1]
    here = here_ref[0]

    def place(offset, tile):
        for v in range(out_ref.shape[0]):
            out_ref[v, here ^ offset] = tile

    for ref, offsets in zip(rest[len(late) : -1], groups, strict=True):
        for j, offset in enumerate(offsets):
            place(offset, ref[j])
    for offset, tile in zip(late, pool_tiles(labels_ref, refs_ref, rest[: len(late)]), strict=True):
        place(offset, tile)


def pool_cost(refs, queries):
    count = sum(q.shape[0] for q in queries)
    return pl.CostEstimate(
        flops=2 * refs.size * count,
        bytes_accessed=refs.size,
        transcendentals=refs.size // S * count,
    )


def pool(labels, refs, queries):
    windows = refs.shape[1] // S
    rows = queries[0].shape[0]
    return pl.pallas_call(
        pool_body,
        out_shape=pltpu.VMEM((len(queries), A, windows * rows), jnp.float32),
        in_specs=[smem] + [vmem] * (1 + len(queries)),
        out_specs=vmem,
        cost_estimate=pool_cost(refs, queries),
        compiler_params=pltpu.CompilerParams(vmem_limit_bytes=40 << 20),
        name="pool",
    )(labels, refs, *queries)


def pool_last(labels, refs, queries, late, tiles, groups, win, count):
    windows = refs.shape[1] // S
    rows = queries[0].shape[0]
    here = lax.axis_index("ref").astype(jnp.int32).reshape(1)
    return pl.pallas_call(
        functools.partial(last_body, late, groups),
        out_shape=pltpu.VMEM((win, count, A, windows * rows), jnp.float32),
        in_specs=[smem, smem] + [vmem] * (1 + len(queries) + len(tiles)),
        out_specs=vmem,
        cost_estimate=pool_cost(refs, queries),
        compiler_params=pltpu.CompilerParams(vmem_limit_bytes=40 << 20),
        name="pool_last",
    )(here, labels, refs, *queries, *tiles)


def finish_body(win, refs, windows, place_ref, taps_ref, bias_ref, in_ref, out_ref):
    here = place_ref[0]
    rows = out_ref.shape[2]

    def centered(block):
        parts = in_ref[pl.ds(block * refs, refs)]
        highest = jnp.max(parts, axis=0)
        pooled = highest + jnp.log(jnp.sum(jnp.exp(parts - highest[None]), axis=0))
        return pooled - jnp.mean(pooled, axis=0, keepdims=True)

    before = jnp.where(here > 0, centered(jnp.maximum(here - 1, 0)), 0.0)
    after = jnp.where(here < win - 1, centered(jnp.minimum(here + 1, win - 1)), 0.0)
    padded = jnp.concatenate([before, centered(here), after], axis=1)
    width = windows * rows
    total = jnp.zeros((A, width), jnp.float32)
    for tap in range(TAPS):
        start = width + (tap - HALF) * rows
        total = total + taps_ref[:, tap : tap + 1] * padded[:, start : start + width]
    same = lax.broadcasted_iota(jnp.int32, (A, A), 0) == lax.broadcasted_iota(jnp.int32, (A, A), 1)
    logits = total + jnp.sum(jnp.where(same, bias_ref[...], 0.0), axis=1, keepdims=True)
    shifted = logits - jnp.max(logits, axis=0, keepdims=True)
    result = shifted - jnp.log(jnp.sum(jnp.exp(shifted), axis=0, keepdims=True))
    for window in range(windows):
        out_ref[window] = result[:, window * rows : (window + 1) * rows]


def finish(received, kernel, class_bias, win, refs, windows, rows):
    place = lax.axis_index("win").astype(jnp.int32).reshape(1)
    operands = [
        pltpu.with_memory_space_constraint(x, pltpu.VMEM)
        for x in (kernel.T, class_bias[None, :], received)
    ]
    return pl.pallas_call(
        functools.partial(finish_body, win, refs, windows),
        out_shape=jax.ShapeDtypeStruct((windows, A, rows), jnp.float32),
        in_specs=[smem] + [vmem] * 3,
        out_specs=vmem,
        name="finish",
    )(place, *operands)


def exchange(block, offset, size):
    return lax.ppermute(block, "ref", [(i, i ^ offset) for i in range(size)])


def tie_body(*refs):
    pass


def tie(value, *others):
    return pl.pallas_call(
        tie_body,
        out_shape=pltpu.VMEM(value.shape, value.dtype),
        in_specs=[vmem] * (1 + len(others)),
        out_specs=vmem,
        input_output_aliases={0: 0},
        compiler_params=pltpu.CompilerParams(vmem_limit_bytes=40 << 20),
        name="tie",
    )(value, *others)


def gather_queries(queries, mine, size, early):
    bits = [1 << b for b in range(1, size.bit_length() - 1)][::-1]
    blocks = {0: mine}
    for bit in bits[:-1] + [1]:
        blocks[bit] = exchange(mine if bit <= 2 else queries, bit, size)
    blocks[2] = exchange(tie(mine, blocks[1]), 2, size)
    pooled = early(blocks)
    even = [0]
    for bit in bits:
        for k in list(even):
            if k:
                blocks[k | bit] = exchange(blocks[k], bit, size)
            even.append(k | bit)
    for k in even[1:]:
        if k == 2:
            blocks[k | 1] = exchange(blocks[1], k, size)
        else:
            blocks[k | 1] = exchange(blocks[k], 1, size)
        if (k // 2) % 4 == 0:
            early(blocks)
    return blocks


def per_device(queries, references, labels, kernel, class_bias):
    refs, win = lax.axis_size("ref"), lax.axis_size("win")
    windows = references.shape[1] // S
    rows = queries.shape[0]
    staged, mine = stage(references, queries)
    tiles, groups = [], []

    def early(blocks):
        groups.append([k for k in blocks if k not in sum(groups, [])])
        tiles.append(pool(labels, staged, [blocks[k] for k in groups[-1]]))
        return tiles[-1]

    blocks = gather_queries(queries, mine, refs, early)
    late = [k for k in blocks if k not in sum(groups, [])]
    sent = pool_last(labels, staged, [blocks[k] for k in late], late, tiles, groups, win, refs)
    sent = sent.reshape((win * refs,) + sent.shape[2:])
    received = lax.all_to_all(sent, ("win", "ref"), split_axis=0, concat_axis=0, tiled=True)
    return finish(received, kernel, class_bias, win, refs, windows, rows)


def solution(mesh):
    in_specs = (P("ref", "win"), P("ref", "win"), P("ref"), P(), P())
    out_specs = P("win", None, "ref")
    return jax.shard_map(
        per_device, mesh=mesh, in_specs=in_specs, out_specs=out_specs, check_vma=False
    )
```

```python
import functools

import jax
import jax.numpy as jnp
from jax import lax
from jax.experimental import pallas as pl
from jax.experimental.pallas import tpu as pltpu
from jax.sharding import PartitionSpec as P

S = 512
A = 8
BLOCK = 128
TAPS = 9
HALF = TAPS // 2
LAST = 4

LOG2E = 1.4426950408889634
SCALE = 256.0 / S

neg_floor = -1e30
narrow = jnp.float8_e4m3fn
vmem = pl.BlockSpec(memory_space=pltpu.VMEM)
smem = pl.BlockSpec(memory_space=pltpu.SMEM)
anywhere = pl.BlockSpec(memory_space=pl.ANY)


def pool_window(scores, labels_ref):
    count = scores.shape[1]
    blocks = scores.shape[0] // BLOCK
    ancestry = lax.broadcasted_iota(jnp.int32, (A, count), 0)
    peaks, totals = [], []
    for b in range(blocks):
        part = scores[b * BLOCK : (b + 1) * BLOCK]
        peak = jnp.max(part, axis=0, keepdims=True)
        totals.append(jnp.sum(jnp.exp2((part - peak) * (SCALE * LOG2E)), axis=0, keepdims=True))
        peaks.append(peak)
    members = [ancestry == labels_ref[b] for b in range(blocks)]
    group_peak = jnp.full((A, count), neg_floor, jnp.float32)
    for b in range(blocks):
        group_peak = jnp.where(members[b], jnp.maximum(group_peak, peaks[b]), group_peak)
    group_total = jnp.zeros((A, count), jnp.float32)
    for b in range(blocks):
        weight = totals[b] * jnp.exp2((peaks[b] - group_peak) * (SCALE * LOG2E))
        group_total = group_total + jnp.where(members[b], weight, 0.0)
    return jnp.where(group_total > 0, SCALE * group_peak + jnp.log(group_total), neg_floor)


def stage_body(refs_ref, queries_ref, out_ref, mine_ref, chunks, sems):
    count, step = chunks.shape[0], chunks.shape[1]
    copies = [
        pltpu.make_async_copy(refs_ref.at[pl.ds(c * step, step)], chunks.at[c], sems.at[c])
        for c in range(count)
    ]
    copies.append(pltpu.make_async_copy(queries_ref, mine_ref, sems.at[count]))
    for copy in copies:
        copy.start()
    for c in range(count):
        copies[c].wait()
        out_ref[c * step : (c + 1) * step] = chunks[c].astype(narrow)
    copies[count].wait()


def stage(references, queries):
    step = 128
    count = references.shape[0] // step
    return pl.pallas_call(
        stage_body,
        out_shape=(
            pltpu.VMEM(references.shape, narrow),
            pltpu.VMEM(queries.shape, queries.dtype),
        ),
        in_specs=[anywhere] * 2,
        out_specs=(vmem, vmem),
        scratch_shapes=[
            pltpu.VMEM((count, step, references.shape[1]), references.dtype),
            pltpu.SemaphoreType.DMA((count + 1,)),
        ],
        cost_estimate=pl.CostEstimate(
            flops=references.size, bytes_accessed=3 * references.size, transcendentals=0
        ),
        compiler_params=pltpu.CompilerParams(vmem_limit_bytes=40 << 20),
        name="stage",
    )(*(pltpu.with_memory_space_constraint(x, pltpu.HBM) for x in (references, queries)))


def pool_tiles(labels_ref, refs_ref, query_refs):
    windows = refs_ref.shape[1] // S
    rows = query_refs[0].shape[0]
    pooled = []
    for window in range(windows):
        cols = slice(window * S, (window + 1) * S)
        queries = jnp.concatenate([q[:, cols] for q in query_refs], axis=0)
        scores = lax.dot_general(
            refs_ref[:, cols],
            queries.astype(narrow),
            (((1,), (1,)), ((), ())),
            preferred_element_type=jnp.float32,
        )
        pooled.append(pool_window(scores, labels_ref))
    return [
        jnp.concatenate([p[:, j * rows : (j + 1) * rows] for p in pooled], axis=1)
        for j in range(len(query_refs))
    ]


def pool_body(labels_ref, refs_ref, *rest):
    out_ref = rest[-1]
    for j, tile in enumerate(pool_tiles(labels_ref, refs_ref, rest[:-1])):
        out_ref[j] = tile


def last_body(late, groups, here_ref, labels_ref, refs_ref, *rest):
    out_ref = rest[-1]
    here = here_ref[0]

    def place(offset, tile):
        for v in range(out_ref.shape[0]):
            out_ref[v, here ^ offset] = tile

    for ref, offsets in zip(rest[len(late) : -1], groups, strict=True):
        for j, offset in enumerate(offsets):
            place(offset, ref[j])
    for offset, tile in zip(late, pool_tiles(labels_ref, refs_ref, rest[: len(late)]), strict=True):
        place(offset, tile)


def pool_cost(refs, queries):
    count = sum(q.shape[0] for q in queries)
    return pl.CostEstimate(
        flops=2 * refs.size * count,
        bytes_accessed=refs.size,
        transcendentals=refs.size // S * count,
    )


def pool(labels, refs, queries):
    windows = refs.shape[1] // S
    rows = queries[0].shape[0]
    return pl.pallas_call(
        pool_body,
        out_shape=pltpu.VMEM((len(queries), A, windows * rows), jnp.float32),
        in_specs=[smem] + [vmem] * (1 + len(queries)),
        out_specs=vmem,
        cost_estimate=pool_cost(refs, queries),
        compiler_params=pltpu.CompilerParams(vmem_limit_bytes=40 << 20),
        name="pool",
    )(labels, refs, *queries)


def pool_last(labels, refs, queries, late, tiles, groups, win, count):
    windows = refs.shape[1] // S
    rows = queries[0].shape[0]
    here = lax.axis_index("ref").astype(jnp.int32).reshape(1)
    return pl.pallas_call(
        functools.partial(last_body, late, groups),
        out_shape=pltpu.VMEM((win, count, A, windows * rows), jnp.float32),
        in_specs=[smem, smem] + [vmem] * (1 + len(queries) + len(tiles)),
        out_specs=vmem,
        cost_estimate=pool_cost(refs, queries),
        compiler_params=pltpu.CompilerParams(vmem_limit_bytes=40 << 20),
        name="pool_last",
    )(here, labels, refs, *queries, *tiles)


def finish_body(win, refs, windows, place_ref, taps_ref, bias_ref, in_ref, out_ref):
    here = place_ref[0]
    rows = out_ref.shape[2]

    def centered(block):
        parts = in_ref[pl.ds(block * refs, refs)]
        highest = jnp.max(parts, axis=0)
        pooled = highest + jnp.log(jnp.sum(jnp.exp(parts - highest[None]), axis=0))
        return pooled - jnp.mean(pooled, axis=0, keepdims=True)

    before = jnp.where(here > 0, centered(jnp.maximum(here - 1, 0)), 0.0)
    after = jnp.where(here < win - 1, centered(jnp.minimum(here + 1, win - 1)), 0.0)
    padded = jnp.concatenate([before, centered(here), after], axis=1)
    width = windows * rows
    total = jnp.zeros((A, width), jnp.float32)
    for tap in range(TAPS):
        start = width + (tap - HALF) * rows
        total = total + taps_ref[:, tap : tap + 1] * padded[:, start : start + width]
    same = lax.broadcasted_iota(jnp.int32, (A, A), 0) == lax.broadcasted_iota(jnp.int32, (A, A), 1)
    logits = total + jnp.sum(jnp.where(same, bias_ref[...], 0.0), axis=1, keepdims=True)
    shifted = logits - jnp.max(logits, axis=0, keepdims=True)
    result = shifted - jnp.log(jnp.sum(jnp.exp(shifted), axis=0, keepdims=True))
    for window in range(windows):
        out_ref[window] = result[:, window * rows : (window + 1) * rows]


def finish(received, kernel, class_bias, win, refs, windows, rows):
    place = lax.axis_index("win").astype(jnp.int32).reshape(1)
    operands = [
        pltpu.with_memory_space_constraint(x, pltpu.VMEM)
        for x in (kernel.T, class_bias[None, :], received)
    ]
    return pl.pallas_call(
        functools.partial(finish_body, win, refs, windows),
        out_shape=jax.ShapeDtypeStruct((windows, A, rows), jnp.float32),
        in_specs=[smem] + [vmem] * 3,
        out_specs=vmem,
        name="finish",
    )(place, *operands)


def exchange(block, offset, size):
    return lax.ppermute(block, "ref", [(i, i ^ offset) for i in range(size)])


def tie_body(*refs):
    pass


def tie(value, *others):
    return pl.pallas_call(
        tie_body,
        out_shape=pltpu.VMEM(value.shape, value.dtype),
        in_specs=[anywhere] * (1 + len(others)),
        out_specs=anywhere,
        input_output_aliases={0: 0},
        name="tie",
    )(value, *(pltpu.with_memory_space_constraint(x, pltpu.VMEM) for x in others))


def gather_queries(queries, mine, size, early):
    far = [k for k in range(4, size, 2)]
    blocks = {0: mine}
    for k in [k for k in far if k & 2]:
        blocks[k] = exchange(queries, k, size)
    blocks[1] = exchange(mine, 1, size)
    blocks[2] = exchange(mine, 2, size)
    first = [0, 1, 2, far[-1]]
    pooled = early({k: blocks[k] for k in first})
    for k in [k for k in far if not k & 2]:
        blocks[k] = exchange(blocks[k | 2], 2, size)
    for k in far:
        source = tie(blocks[k], pooled) if k == 4 else blocks[k]
        blocks[k | 1] = exchange(source, 1, size)
    blocks[3] = exchange(blocks[1], 2, size)
    rest = [k for k in blocks if k not in first]
    for k in range(0, len(rest) - LAST, LAST):
        early({j: blocks[j] for j in rest[k : k + LAST]})
    return blocks


def per_device(queries, references, labels, kernel, class_bias):
    refs, win = lax.axis_size("ref"), lax.axis_size("win")
    windows = references.shape[1] // S
    rows = queries.shape[0]
    staged, mine = stage(references, queries)
    tiles, groups = [], []

    def early(blocks):
        groups.append(list(blocks))
        tiles.append(pool(labels, staged, list(blocks.values())))
        return tiles[-1]

    blocks = gather_queries(queries, mine, refs, early)
    late = [k for k in blocks if k not in sum(groups, [])]
    sent = pool_last(labels, staged, [blocks[k] for k in late], late, tiles, groups, win, refs)
    sent = sent.reshape((win * refs,) + sent.shape[2:])
    received = lax.all_to_all(sent, ("win", "ref"), split_axis=0, concat_axis=0, tiled=True)
    return finish(received, kernel, class_bias, win, refs, windows, rows)


def solution(mesh):
    in_specs = (P("ref", "win"), P("ref", "win"), P("ref"), P(), P())
    out_specs = P("win", None, "ref")
    return jax.shard_map(
        per_device, mesh=mesh, in_specs=in_specs, out_specs=out_specs, check_vma=False
    )
```

```python
import functools

import jax
import jax.numpy as jnp
from jax import lax
from jax.experimental import pallas as pl
from jax.experimental.pallas import tpu as pltpu
from jax.sharding import PartitionSpec as P

S = 512
A = 8
BLOCK = 128
TAPS = 9
HALF = TAPS // 2
LAST = 4

LOG2E = 1.4426950408889634
SCALE = 256.0 / S

neg_floor = -1e30
narrow = jnp.float8_e4m3fn
vmem = pl.BlockSpec(memory_space=pltpu.VMEM)
anywhere = pl.BlockSpec(memory_space=pl.ANY)


def pool_window(scores, members):
    count = scores.shape[1]
    blocks = scores.shape[0] // BLOCK
    peaks, totals = [], []
    for b in range(blocks):
        part = scores[b * BLOCK : (b + 1) * BLOCK]
        peak = jnp.max(part, axis=0, keepdims=True)
        totals.append(jnp.sum(jnp.exp2((part - peak) * (SCALE * LOG2E)), axis=0, keepdims=True))
        peaks.append(peak)
    group_peak = jnp.full((A, count), neg_floor, jnp.float32)
    for b in range(blocks):
        group_peak = jnp.where(members[b], jnp.maximum(group_peak, peaks[b]), group_peak)
    group_total = jnp.zeros((A, count), jnp.float32)
    for b in range(blocks):
        weight = totals[b] * jnp.exp2((peaks[b] - group_peak) * (SCALE * LOG2E))
        group_total = group_total + jnp.where(members[b], weight, 0.0)
    return jnp.where(group_total > 0, SCALE * group_peak + jnp.log(group_total), neg_floor)


def stage_body(
    refs_ref, queries_ref, labels_in, taps_in, bias_in,
    out_ref, mine_ref, members_ref, consts_ref,
    chunks, labels_ref, taps_ref, bias_ref, sems,
):
    count, step = chunks.shape[0], chunks.shape[1]
    copies = [
        pltpu.make_async_copy(refs_ref.at[pl.ds(c * step, step)], chunks.at[c], sems.at[c])
        for c in range(count)
    ]
    small = [(labels_in, labels_ref), (taps_in, taps_ref), (bias_in, bias_ref)]
    small.append((queries_ref, mine_ref))
    for source, target in small:
        copies.append(pltpu.make_async_copy(source, target, sems.at[len(copies)]))
    for copy in copies[count:] + copies[:count]:
        copy.start()
    for copy in copies[count:]:
        copy.wait()
    ancestry = lax.broadcasted_iota(jnp.int32, (A, BLOCK), 0)
    for b in range(members_ref.shape[0]):
        members_ref[b] = (ancestry == labels_ref[b]).astype(jnp.float32)
    same = lax.broadcasted_iota(jnp.int32, (A, A), 0) == lax.broadcasted_iota(jnp.int32, (A, A), 1)
    bias = jnp.sum(jnp.where(same, bias_ref[...], 0.0), axis=1, keepdims=True)
    for tap in range(TAPS):
        consts_ref[tap] = jnp.broadcast_to(taps_ref[:, tap : tap + 1], (A, BLOCK))
    consts_ref[TAPS] = jnp.broadcast_to(bias, (A, BLOCK))
    for c in range(count):
        copies[c].wait()
        out_ref[c * step : (c + 1) * step] = chunks[c].astype(narrow)


def stage(references, queries, labels, kernel, class_bias):
    step = 128
    count = references.shape[0] // step
    operands = (references, queries, labels, kernel.T, class_bias[None, :])
    return pl.pallas_call(
        stage_body,
        out_shape=(
            pltpu.VMEM(references.shape, narrow),
            pltpu.VMEM(queries.shape, queries.dtype),
            pltpu.VMEM((references.shape[0] // BLOCK, A, BLOCK), jnp.float32),
            pltpu.VMEM((TAPS + 1, A, BLOCK), jnp.float32),
        ),
        in_specs=[anywhere] * len(operands),
        out_specs=(vmem,) * 4,
        scratch_shapes=[
            pltpu.VMEM((count, step, references.shape[1]), references.dtype),
            pltpu.SMEM(labels.shape, labels.dtype),
            pltpu.VMEM((A, TAPS), kernel.dtype),
            pltpu.VMEM((1, A), class_bias.dtype),
            pltpu.SemaphoreType.DMA((count + 4,)),
        ],
        cost_estimate=pl.CostEstimate(
            flops=references.size, bytes_accessed=3 * references.size, transcendentals=0
        ),
        compiler_params=pltpu.CompilerParams(vmem_limit_bytes=40 << 20),
        name="stage",
    )(*(pltpu.with_memory_space_constraint(x, pltpu.HBM) for x in operands))


def pool_tiles(members_ref, refs_ref, query_refs):
    windows = refs_ref.shape[1] // S
    rows = query_refs[0].shape[0]
    count = rows * len(query_refs)
    members = [members_ref[b] > 0.5 for b in range(members_ref.shape[0])]
    if count != BLOCK:
        members = [
            jnp.broadcast_to(members_ref[b][:, :1], (A, count)) > 0.5 for b in range(len(members))
        ]
    pooled = []
    for window in range(windows):
        cols = slice(window * S, (window + 1) * S)
        queries = jnp.concatenate([q[:, cols] for q in query_refs], axis=0)
        scores = lax.dot_general(
            refs_ref[:, cols],
            queries.astype(narrow),
            (((1,), (1,)), ((), ())),
            preferred_element_type=jnp.float32,
        )
        pooled.append(pool_window(scores, members))
    return [
        jnp.concatenate([p[:, j * rows : (j + 1) * rows] for p in pooled], axis=1)
        for j in range(len(query_refs))
    ]


def pool_body(members_ref, refs_ref, *rest):
    out_ref = rest[-1]
    for j, tile in enumerate(pool_tiles(members_ref, refs_ref, rest[:-1])):
        out_ref[j] = tile


def last_body(late, groups, members_ref, refs_ref, *rest):
    out_ref = rest[-1]
    here = lax.axis_index("ref")

    def place(offset, tile):
        for v in range(out_ref.shape[0]):
            out_ref[v, here ^ offset] = tile

    for ref, offsets in zip(rest[len(late) : -1], groups, strict=True):
        for j, offset in enumerate(offsets):
            place(offset, ref[j])
    for offset, tile in zip(late, pool_tiles(members_ref, refs_ref, rest[: len(late)]), strict=True):
        place(offset, tile)


def pool_cost(refs, queries):
    count = sum(q.shape[0] for q in queries)
    return pl.CostEstimate(
        flops=2 * refs.size * count,
        bytes_accessed=refs.size,
        transcendentals=refs.size // S * count,
    )


def pool(members, refs, queries):
    windows = refs.shape[1] // S
    rows = queries[0].shape[0]
    return pl.pallas_call(
        pool_body,
        out_shape=pltpu.VMEM((len(queries), A, windows * rows), jnp.float32),
        in_specs=[vmem] * (2 + len(queries)),
        out_specs=vmem,
        cost_estimate=pool_cost(refs, queries),
        compiler_params=pltpu.CompilerParams(vmem_limit_bytes=40 << 20),
        name="pool",
    )(members, refs, *queries)


def pool_last(members, refs, queries, late, tiles, groups, win, count):
    windows = refs.shape[1] // S
    rows = queries[0].shape[0]
    return pl.pallas_call(
        functools.partial(last_body, late, groups),
        out_shape=pltpu.VMEM((win, count, A, windows * rows), jnp.float32),
        in_specs=[vmem] * (2 + len(queries) + len(tiles)),
        out_specs=vmem,
        cost_estimate=pool_cost(refs, queries),
        compiler_params=pltpu.CompilerParams(vmem_limit_bytes=40 << 20),
        name="pool_last",
    )(members, refs, *queries, *tiles)


def finish_body(win, refs, windows, consts_ref, in_ref, out_ref):
    here = lax.axis_index("win")
    rows = out_ref.shape[2]

    def centered(block):
        parts = in_ref[pl.ds(block * refs, refs)]
        highest = jnp.max(parts, axis=0)
        pooled = highest + jnp.log(jnp.sum(jnp.exp(parts - highest[None]), axis=0))
        return pooled - jnp.mean(pooled, axis=0, keepdims=True)

    before = jnp.where(here > 0, centered(jnp.maximum(here - 1, 0)), 0.0)
    after = jnp.where(here < win - 1, centered(jnp.minimum(here + 1, win - 1)), 0.0)
    padded = jnp.concatenate([before, centered(here), after], axis=1)
    width = windows * rows
    total = jnp.zeros((A, width), jnp.float32)
    for tap in range(TAPS):
        start = width + (tap - HALF) * rows
        total = total + consts_ref[tap][:, :width] * padded[:, start : start + width]
    logits = total + consts_ref[TAPS][:, :width]
    shifted = logits - jnp.max(logits, axis=0, keepdims=True)
    result = shifted - jnp.log(jnp.sum(jnp.exp(shifted), axis=0, keepdims=True))
    for window in range(windows):
        out_ref[window] = result[:, window * rows : (window + 1) * rows]


def finish(received, consts, win, refs, windows, rows):
    return pl.pallas_call(
        functools.partial(finish_body, win, refs, windows),
        out_shape=jax.ShapeDtypeStruct((windows, A, rows), jnp.float32),
        in_specs=[vmem] * 2,
        out_specs=vmem,
        name="finish",
    )(*(pltpu.with_memory_space_constraint(x, pltpu.VMEM) for x in (consts, received)))


def exchange(block, offset, size):
    return lax.ppermute(block, "ref", [(i, i ^ offset) for i in range(size)])


def tie_body(*refs):
    pass


def tie(value, *others):
    return pl.pallas_call(
        tie_body,
        out_shape=pltpu.VMEM(value.shape, value.dtype),
        in_specs=[anywhere] * (1 + len(others)),
        out_specs=anywhere,
        input_output_aliases={0: 0},
        name="tie",
    )(value, *(pltpu.with_memory_space_constraint(x, pltpu.VMEM) for x in others))


def gather_queries(queries, mine, size, early):
    far = [k for k in range(4, size, 2)]
    blocks = {0: mine}
    for k in [k for k in far if k & 2]:
        blocks[k] = exchange(queries, k, size)
    blocks[1] = exchange(mine, 1, size)
    blocks[2] = exchange(mine, 2, size)
    first = [0, 1, 2, far[-1]]
    pooled = early({k: blocks[k] for k in first})
    for k in [k for k in far if not k & 2]:
        blocks[k] = exchange(blocks[k | 2], 2, size)
    for k in far:
        source = tie(blocks[k], pooled) if k == 4 else blocks[k]
        blocks[k | 1] = exchange(source, 1, size)
    blocks[3] = exchange(blocks[1], 2, size)
    rest = [k for k in blocks if k not in first]
    for k in range(0, len(rest) - LAST, LAST):
        early({j: blocks[j] for j in rest[k : k + LAST]})
    return blocks


def per_device(queries, references, labels, kernel, class_bias):
    refs, win = lax.axis_size("ref"), lax.axis_size("win")
    windows = references.shape[1] // S
    rows = queries.shape[0]
    staged, mine, members, consts = stage(references, queries, labels, kernel, class_bias)
    tiles, groups = [], []

    def early(blocks):
        groups.append(list(blocks))
        tiles.append(pool(members, staged, list(blocks.values())))
        return tiles[-1]

    blocks = gather_queries(queries, mine, refs, early)
    late = [k for k in blocks if k not in sum(groups, [])]
    sent = pool_last(members, staged, [blocks[k] for k in late], late, tiles, groups, win, refs)
    sent = sent.reshape((win * refs,) + sent.shape[2:])
    received = lax.all_to_all(sent, ("win", "ref"), split_axis=0, concat_axis=0, tiled=True)
    return finish(received, consts, win, refs, windows, rows)


def solution(mesh):
    in_specs = (P("ref", "win"), P("ref", "win"), P("ref"), P(), P())
    out_specs = P("win", None, "ref")
    return jax.shard_map(
        per_device, mesh=mesh, in_specs=in_specs, out_specs=out_specs, check_vma=False
    )
```

```python
import functools

import jax
import jax.numpy as jnp
from jax import lax
from jax.experimental import pallas as pl
from jax.experimental.pallas import tpu as pltpu
from jax.sharding import PartitionSpec as P

S = 512
A = 8
BLOCK = 128
TAPS = 9
HALF = TAPS // 2
LAST = 4

LOG2E = 1.4426950408889634
SCALE = 256.0 / S

neg_floor = -1e30
narrow = jnp.float8_e4m3fn
vmem = pl.BlockSpec(memory_space=pltpu.VMEM)
anywhere = pl.BlockSpec(memory_space=pl.ANY)


def pool_window(scores, members):
    count = scores.shape[1]
    blocks = scores.shape[0] // BLOCK
    peaks, totals = [], []
    for b in range(blocks):
        part = scores[b * BLOCK : (b + 1) * BLOCK]
        peak = jnp.max(part, axis=0, keepdims=True)
        totals.append(jnp.sum(jnp.exp2((part - peak) * (SCALE * LOG2E)), axis=0, keepdims=True))
        peaks.append(peak)
    group_peak = jnp.full((A, count), neg_floor, jnp.float32)
    for b in range(blocks):
        group_peak = jnp.where(members[b], jnp.maximum(group_peak, peaks[b]), group_peak)
    group_total = jnp.zeros((A, count), jnp.float32)
    for b in range(blocks):
        weight = totals[b] * jnp.exp2((peaks[b] - group_peak) * (SCALE * LOG2E))
        group_total = group_total + jnp.where(members[b], weight, 0.0)
    return jnp.where(group_total > 0, SCALE * group_peak + jnp.log(group_total), neg_floor)


def stage_body(
    refs_ref, queries_ref, labels_in, taps_in, bias_in,
    out_ref, mine_ref, members_ref, consts_ref,
    chunks, labels_ref, taps_ref, bias_ref, sems,
):
    count, step = chunks.shape[0], chunks.shape[1]
    copies = [
        pltpu.make_async_copy(refs_ref.at[pl.ds(c * step, step)], chunks.at[c], sems.at[c])
        for c in range(count)
    ]
    small = [(labels_in, labels_ref), (taps_in, taps_ref), (bias_in, bias_ref)]
    small.append((queries_ref, mine_ref))
    for source, target in small:
        copies.append(pltpu.make_async_copy(source, target, sems.at[len(copies)]))
    for copy in copies[count:] + copies[:count]:
        copy.start()
    for copy in copies[count:]:
        copy.wait()
    ancestry = lax.broadcasted_iota(jnp.int32, (A, BLOCK), 0)
    for b in range(members_ref.shape[0]):
        members_ref[b] = (ancestry == labels_ref[b]).astype(jnp.float32)
    same = lax.broadcasted_iota(jnp.int32, (A, A), 0) == lax.broadcasted_iota(jnp.int32, (A, A), 1)
    bias = jnp.sum(jnp.where(same, bias_ref[...], 0.0), axis=1, keepdims=True)
    for tap in range(TAPS):
        consts_ref[tap] = jnp.broadcast_to(taps_ref[:, tap : tap + 1], (A, BLOCK))
    consts_ref[TAPS] = jnp.broadcast_to(bias, (A, BLOCK))
    for c in range(count):
        copies[c].wait()
        out_ref[c * step : (c + 1) * step] = chunks[c].astype(narrow)


def stage(references, queries, labels, kernel, class_bias):
    step = 128
    count = references.shape[0] // step
    operands = (references, queries, labels, kernel.T, class_bias[None, :])
    return pl.pallas_call(
        stage_body,
        out_shape=(
            pltpu.VMEM(references.shape, narrow),
            pltpu.VMEM(queries.shape, queries.dtype),
            pltpu.VMEM((references.shape[0] // BLOCK, A, BLOCK), jnp.float32),
            pltpu.VMEM((TAPS + 1, A, BLOCK), jnp.float32),
        ),
        in_specs=[anywhere] * len(operands),
        out_specs=(vmem,) * 4,
        scratch_shapes=[
            pltpu.VMEM((count, step, references.shape[1]), references.dtype),
            pltpu.SMEM(labels.shape, labels.dtype),
            pltpu.VMEM((A, TAPS), kernel.dtype),
            pltpu.VMEM((1, A), class_bias.dtype),
            pltpu.SemaphoreType.DMA((count + 4,)),
        ],
        cost_estimate=pl.CostEstimate(
            flops=references.size, bytes_accessed=3 * references.size, transcendentals=0
        ),
        compiler_params=pltpu.CompilerParams(vmem_limit_bytes=40 << 20),
        name="stage",
    )(*(pltpu.with_memory_space_constraint(x, pltpu.HBM) for x in operands))


def pool_tiles(members_ref, refs_ref, query_refs):
    windows = refs_ref.shape[1] // S
    rows = query_refs[0].shape[0]
    count = rows * len(query_refs)
    members = [members_ref[b] > 0.5 for b in range(members_ref.shape[0])]
    if count != BLOCK:
        members = [
            jnp.broadcast_to(members_ref[b][:, :1], (A, count)) > 0.5 for b in range(len(members))
        ]
    pooled = []
    for window in range(windows):
        cols = slice(window * S, (window + 1) * S)
        queries = jnp.concatenate([q[:, cols] for q in query_refs], axis=0)
        scores = lax.dot_general(
            refs_ref[:, cols],
            queries.astype(narrow),
            (((1,), (1,)), ((), ())),
            preferred_element_type=jnp.float32,
        )
        pooled.append(pool_window(scores, members))
    return [
        jnp.concatenate([p[:, j * rows : (j + 1) * rows] for p in pooled], axis=1)
        for j in range(len(query_refs))
    ]


def pool_body(members_ref, refs_ref, *rest):
    out_ref = rest[-1]
    for j, tile in enumerate(pool_tiles(members_ref, refs_ref, rest[:-1])):
        out_ref[j] = tile


def last_body(late, groups, members_ref, refs_ref, *rest):
    out_ref = rest[-1]
    here = lax.axis_index("ref")

    def place(offset, tile):
        for v in range(out_ref.shape[0]):
            out_ref[v, here ^ offset] = tile

    for ref, offsets in zip(rest[len(late) : -1], groups, strict=True):
        for j, offset in enumerate(offsets):
            place(offset, ref[j])
    for offset, tile in zip(late, pool_tiles(members_ref, refs_ref, rest[: len(late)]), strict=True):
        place(offset, tile)


def pool_cost(refs, queries):
    count = sum(q.shape[0] for q in queries)
    return pl.CostEstimate(
        flops=2 * refs.size * count,
        bytes_accessed=refs.size,
        transcendentals=refs.size // S * count,
    )


def pool(members, refs, queries):
    windows = refs.shape[1] // S
    rows = queries[0].shape[0]
    return pl.pallas_call(
        pool_body,
        out_shape=pltpu.VMEM((len(queries), A, windows * rows), jnp.float32),
        in_specs=[vmem] * (2 + len(queries)),
        out_specs=vmem,
        cost_estimate=pool_cost(refs, queries),
        compiler_params=pltpu.CompilerParams(vmem_limit_bytes=40 << 20),
        name="pool",
    )(members, refs, *queries)


def pool_last(members, refs, queries, late, tiles, groups, win, count):
    windows = refs.shape[1] // S
    rows = queries[0].shape[0]
    return pl.pallas_call(
        functools.partial(last_body, late, groups),
        out_shape=pltpu.VMEM((win, count, A, windows * rows), jnp.float32),
        in_specs=[vmem] * (2 + len(queries) + len(tiles)),
        out_specs=vmem,
        cost_estimate=pool_cost(refs, queries),
        compiler_params=pltpu.CompilerParams(vmem_limit_bytes=40 << 20),
        name="pool_last",
    )(members, refs, *queries, *tiles)


def finish_body(win, refs, windows, consts_ref, in_ref, out_ref):
    here = lax.axis_index("win")
    rows = out_ref.shape[2]

    def centered(block):
        parts = in_ref[pl.ds(block * refs, refs)]
        highest = jnp.max(parts, axis=0)
        pooled = highest + jnp.log(jnp.sum(jnp.exp(parts - highest[None]), axis=0))
        return pooled - jnp.mean(pooled, axis=0, keepdims=True)

    before = jnp.where(here > 0, centered(jnp.maximum(here - 1, 0)), 0.0)
    after = jnp.where(here < win - 1, centered(jnp.minimum(here + 1, win - 1)), 0.0)
    padded = jnp.concatenate([before, centered(here), after], axis=1)
    width = windows * rows
    total = jnp.zeros((A, width), jnp.float32)
    for tap in range(TAPS):
        start = width + (tap - HALF) * rows
        total = total + consts_ref[tap][:, :width] * padded[:, start : start + width]
    logits = total + consts_ref[TAPS][:, :width]
    shifted = logits - jnp.max(logits, axis=0, keepdims=True)
    result = shifted - jnp.log(jnp.sum(jnp.exp(shifted), axis=0, keepdims=True))
    for window in range(windows):
        out_ref[window] = result[:, window * rows : (window + 1) * rows]


def finish(received, consts, win, refs, windows, rows):
    return pl.pallas_call(
        functools.partial(finish_body, win, refs, windows),
        out_shape=jax.ShapeDtypeStruct((windows, A, rows), jnp.float32),
        in_specs=[vmem] * 2,
        out_specs=vmem,
        name="finish",
    )(*(pltpu.with_memory_space_constraint(x, pltpu.VMEM) for x in (consts, received)))


def exchange(block, offset, size):
    return lax.ppermute(block, "ref", [(i, i ^ offset) for i in range(size)])


def gather_queries(queries, mine, size, early):
    near = [k for k in range(4, size, 2) if k & 2]
    blocks = {0: mine}
    for k in near + [2, 1]:
        blocks[k] = exchange(queries, k, size)
    first = [0, 1, 2, near[-1]]
    early({k: blocks[k] for k in first})
    for k in near:
        blocks[k ^ 3] = exchange(mine, k ^ 3, size)
    for k in near:
        blocks[k | 1] = exchange(blocks[k], 1, size)
    for k in near:
        blocks[k ^ 2] = exchange(blocks[k], 2, size)
    blocks[3] = exchange(blocks[2], 1, size)
    rest = [k for k in blocks if k not in first]
    for k in range(0, len(rest) - LAST, LAST):
        early({j: blocks[j] for j in rest[k : k + LAST]})
    return blocks


def per_device(queries, references, labels, kernel, class_bias):
    refs, win = lax.axis_size("ref"), lax.axis_size("win")
    windows = references.shape[1] // S
    rows = queries.shape[0]
    staged, mine, members, consts = stage(references, queries, labels, kernel, class_bias)
    tiles, groups = [], []

    def early(blocks):
        groups.append(list(blocks))
        tiles.append(pool(members, staged, list(blocks.values())))
        return tiles[-1]

    blocks = gather_queries(queries, mine, refs, early)
    late = [k for k in blocks if k not in sum(groups, [])]
    sent = pool_last(members, staged, [blocks[k] for k in late], late, tiles, groups, win, refs)
    sent = sent.reshape((win * refs,) + sent.shape[2:])
    received = lax.all_to_all(sent, ("win", "ref"), split_axis=0, concat_axis=0, tiled=True)
    return finish(received, consts, win, refs, windows, rows)


def solution(mesh):
    in_specs = (P("ref", "win"), P("ref", "win"), P("ref"), P(), P())
    out_specs = P("win", None, "ref")
    return jax.shard_map(
        per_device, mesh=mesh, in_specs=in_specs, out_specs=out_specs, check_vma=False
    )
```

```python
import functools

import jax
import jax.numpy as jnp
from jax import lax
from jax.experimental import pallas as pl
from jax.experimental.pallas import tpu as pltpu
from jax.sharding import PartitionSpec as P

S = 512
A = 8
BLOCK = 128
TAPS = 9
HALF = TAPS // 2
LAST = 4

LOG2E = 1.4426950408889634
SCALE = 256.0 / S

neg_floor = -1e30
narrow = jnp.float8_e4m3fn
vmem = pl.BlockSpec(memory_space=pltpu.VMEM)
anywhere = pl.BlockSpec(memory_space=pl.ANY)


def pool_window(scores, members):
    count = scores.shape[1]
    blocks = scores.shape[0] // BLOCK
    peaks, totals = [], []
    for b in range(blocks):
        part = scores[b * BLOCK : (b + 1) * BLOCK]
        peak = jnp.max(part, axis=0, keepdims=True)
        totals.append(jnp.sum(jnp.exp2((part - peak) * (SCALE * LOG2E)), axis=0, keepdims=True))
        peaks.append(peak)
    group_peak = jnp.full((A, count), neg_floor, jnp.float32)
    for b in range(blocks):
        group_peak = jnp.where(members[b], jnp.maximum(group_peak, peaks[b]), group_peak)
    group_total = jnp.zeros((A, count), jnp.float32)
    for b in range(blocks):
        weight = totals[b] * jnp.exp2((peaks[b] - group_peak) * (SCALE * LOG2E))
        group_total = group_total + jnp.where(members[b], weight, 0.0)
    return jnp.where(group_total > 0, SCALE * group_peak + jnp.log(group_total), neg_floor)


def stage_body(
    refs_ref, queries_ref, labels_in, taps_in, bias_in,
    out_ref, mine_ref, members_ref, consts_ref,
    chunks, labels_ref, taps_ref, bias_ref, sems,
):
    count, step = chunks.shape[0], chunks.shape[1]
    copies = [
        pltpu.make_async_copy(refs_ref.at[pl.ds(c * step, step)], chunks.at[c], sems.at[c])
        for c in range(count)
    ]
    small = [(labels_in, labels_ref), (taps_in, taps_ref), (bias_in, bias_ref)]
    small.append((queries_ref, mine_ref))
    for source, target in small:
        copies.append(pltpu.make_async_copy(source, target, sems.at[len(copies)]))
    for copy in copies[count:] + copies[:count]:
        copy.start()
    for copy in copies[count:]:
        copy.wait()
    ancestry = lax.broadcasted_iota(jnp.int32, (A, BLOCK), 0)
    for b in range(members_ref.shape[0]):
        members_ref[b] = (ancestry == labels_ref[b]).astype(jnp.float32)
    same = lax.broadcasted_iota(jnp.int32, (A, A), 0) == lax.broadcasted_iota(jnp.int32, (A, A), 1)
    bias = jnp.sum(jnp.where(same, bias_ref[...], 0.0), axis=1, keepdims=True)
    for tap in range(TAPS):
        consts_ref[tap] = jnp.broadcast_to(taps_ref[:, tap : tap + 1], (A, BLOCK))
    consts_ref[TAPS] = jnp.broadcast_to(bias, (A, BLOCK))
    for c in range(count):
        copies[c].wait()
        out_ref[c * step : (c + 1) * step] = chunks[c].astype(narrow)


def stage(references, queries, labels, kernel, class_bias):
    step = 128
    count = references.shape[0] // step
    operands = (references, queries, labels, kernel.T, class_bias[None, :])
    return pl.pallas_call(
        stage_body,
        out_shape=(
            pltpu.VMEM(references.shape, narrow),
            pltpu.VMEM(queries.shape, queries.dtype),
            pltpu.VMEM((references.shape[0] // BLOCK, A, BLOCK), jnp.float32),
            pltpu.VMEM((TAPS + 1, A, BLOCK), jnp.float32),
        ),
        in_specs=[anywhere] * len(operands),
        out_specs=(vmem,) * 4,
        scratch_shapes=[
            pltpu.VMEM((count, step, references.shape[1]), references.dtype),
            pltpu.SMEM(labels.shape, labels.dtype),
            pltpu.VMEM((A, TAPS), kernel.dtype),
            pltpu.VMEM((1, A), class_bias.dtype),
            pltpu.SemaphoreType.DMA((count + 4,)),
        ],
        cost_estimate=pl.CostEstimate(
            flops=references.size, bytes_accessed=3 * references.size, transcendentals=0
        ),
        compiler_params=pltpu.CompilerParams(vmem_limit_bytes=40 << 20),
        name="stage",
    )(*(pltpu.with_memory_space_constraint(x, pltpu.HBM) for x in operands))


def pool_tiles(members_ref, refs_ref, query_refs):
    windows = refs_ref.shape[1] // S
    rows = query_refs[0].shape[0]
    count = rows * len(query_refs)
    members = [members_ref[b] > 0.5 for b in range(members_ref.shape[0])]
    if count != BLOCK:
        members = [
            jnp.broadcast_to(members_ref[b][:, :1], (A, count)) > 0.5 for b in range(len(members))
        ]
    pooled = []
    for window in range(windows):
        cols = slice(window * S, (window + 1) * S)
        queries = jnp.concatenate([q[:, cols] for q in query_refs], axis=0)
        scores = lax.dot_general(
            refs_ref[:, cols],
            queries.astype(narrow),
            (((1,), (1,)), ((), ())),
            preferred_element_type=jnp.float32,
        )
        pooled.append(pool_window(scores, members))
    return [
        jnp.concatenate([p[:, j * rows : (j + 1) * rows] for p in pooled], axis=1)
        for j in range(len(query_refs))
    ]


def pool_body(members_ref, refs_ref, *rest):
    out_ref = rest[-1]
    for j, tile in enumerate(pool_tiles(members_ref, refs_ref, rest[:-1])):
        out_ref[j] = tile


def last_body(late, groups, members_ref, refs_ref, *rest):
    out_ref = rest[-1]
    here = lax.axis_index("ref")

    def place(offset, tile):
        for v in range(out_ref.shape[0]):
            out_ref[v, here ^ offset] = tile

    for ref, offsets in zip(rest[len(late) : -1], groups, strict=True):
        for j, offset in enumerate(offsets):
            place(offset, ref[j])
    for offset, tile in zip(late, pool_tiles(members_ref, refs_ref, rest[: len(late)]), strict=True):
        place(offset, tile)


def pool_cost(refs, queries):
    count = sum(q.shape[0] for q in queries)
    return pl.CostEstimate(
        flops=2 * refs.size * count,
        bytes_accessed=refs.size,
        transcendentals=refs.size // S * count,
    )


def pool(members, refs, queries):
    windows = refs.shape[1] // S
    rows = queries[0].shape[0]
    return pl.pallas_call(
        pool_body,
        out_shape=pltpu.VMEM((len(queries), A, windows * rows), jnp.float32),
        in_specs=[vmem] * (2 + len(queries)),
        out_specs=vmem,
        cost_estimate=pool_cost(refs, queries),
        compiler_params=pltpu.CompilerParams(vmem_limit_bytes=40 << 20),
        name="pool",
    )(members, refs, *queries)


def pool_last(members, refs, queries, late, tiles, groups, win, count):
    windows = refs.shape[1] // S
    rows = queries[0].shape[0]
    return pl.pallas_call(
        functools.partial(last_body, late, groups),
        out_shape=pltpu.VMEM((win, count, A, windows * rows), jnp.float32),
        in_specs=[vmem] * (2 + len(queries) + len(tiles)),
        out_specs=vmem,
        cost_estimate=pool_cost(refs, queries),
        compiler_params=pltpu.CompilerParams(vmem_limit_bytes=40 << 20),
        name="pool_last",
    )(members, refs, *queries, *tiles)


def finish_body(win, refs, windows, consts_ref, in_ref, out_ref):
    here = lax.axis_index("win")
    rows = out_ref.shape[2]

    def centered(block):
        parts = in_ref[pl.ds(block * refs, refs)]
        highest = jnp.max(parts, axis=0)
        pooled = highest + jnp.log(jnp.sum(jnp.exp(parts - highest[None]), axis=0))
        return pooled - jnp.mean(pooled, axis=0, keepdims=True)

    before = jnp.where(here > 0, centered(jnp.maximum(here - 1, 0)), 0.0)
    after = jnp.where(here < win - 1, centered(jnp.minimum(here + 1, win - 1)), 0.0)
    padded = jnp.concatenate([before, centered(here), after], axis=1)
    width = windows * rows
    total = jnp.zeros((A, width), jnp.float32)
    for tap in range(TAPS):
        start = width + (tap - HALF) * rows
        total = total + consts_ref[tap][:, :width] * padded[:, start : start + width]
    logits = total + consts_ref[TAPS][:, :width]
    shifted = logits - jnp.max(logits, axis=0, keepdims=True)
    result = shifted - jnp.log(jnp.sum(jnp.exp(shifted), axis=0, keepdims=True))
    for window in range(windows):
        out_ref[window] = result[:, window * rows : (window + 1) * rows]


def finish(received, consts, win, refs, windows, rows):
    return pl.pallas_call(
        functools.partial(finish_body, win, refs, windows),
        out_shape=jax.ShapeDtypeStruct((windows, A, rows), jnp.float32),
        in_specs=[vmem] * 2,
        out_specs=vmem,
        name="finish",
    )(*(pltpu.with_memory_space_constraint(x, pltpu.VMEM) for x in (consts, received)))


def exchange(block, offset, size):
    return lax.ppermute(block, "ref", [(i, i ^ offset) for i in range(size)])


def gather_queries(queries, mine, size, early):
    near = [k for k in range(4, size, 2) if k & 2]
    blocks = {0: mine}
    for k in near + [2, 1]:
        blocks[k] = exchange(queries, k, size)
    first = [0, 1, 2, near[-1]]
    early({k: blocks[k] for k in first})
    for k in near:
        blocks[k ^ 3] = exchange(queries, k ^ 3, size)
    for k in near:
        blocks[k | 1] = exchange(blocks[k], 1, size)
    for k in near:
        blocks[k ^ 2] = exchange(blocks[k], 2, size)
    blocks[3] = exchange(blocks[2], 1, size)
    rest = [k for k in blocks if k not in first]
    for k in range(0, len(rest) - LAST, LAST):
        early({j: blocks[j] for j in rest[k : k + LAST]})
    return blocks


def per_device(queries, references, labels, kernel, class_bias):
    refs, win = lax.axis_size("ref"), lax.axis_size("win")
    windows = references.shape[1] // S
    rows = queries.shape[0]
    staged, mine, members, consts = stage(references, queries, labels, kernel, class_bias)
    tiles, groups = [], []

    def early(blocks):
        groups.append(list(blocks))
        tiles.append(pool(members, staged, list(blocks.values())))
        return tiles[-1]

    blocks = gather_queries(queries, mine, refs, early)
    late = [k for k in blocks if k not in sum(groups, [])]
    sent = pool_last(members, staged, [blocks[k] for k in late], late, tiles, groups, win, refs)
    sent = sent.reshape((win * refs,) + sent.shape[2:])
    received = lax.all_to_all(sent, ("win", "ref"), split_axis=0, concat_axis=0, tiled=True)
    return finish(received, consts, win, refs, windows, rows)


def solution(mesh):
    in_specs = (P("ref", "win"), P("ref", "win"), P("ref"), P(), P())
    out_specs = P("win", None, "ref")
    return jax.shard_map(
        per_device, mesh=mesh, in_specs=in_specs, out_specs=out_specs, check_vma=False
    )
```

```python
import functools

import jax
import jax.numpy as jnp
from jax import lax
from jax.experimental import pallas as pl
from jax.experimental.pallas import tpu as pltpu
from jax.sharding import PartitionSpec as P

S = 512
A = 8
BLOCK = 128
TAPS = 9
HALF = TAPS // 2
LAST = 4
PART = 256

LOG2E = 1.4426950408889634
SCALE = 256.0 / S

neg_floor = -1e30
narrow = jnp.float8_e4m3fn
vmem = pl.BlockSpec(memory_space=pltpu.VMEM)
anywhere = pl.BlockSpec(memory_space=pl.ANY)


def pool_window(scores, members):
    count = scores[0].shape[1]
    per = scores[0].shape[0] // BLOCK
    blocks = per * len(scores)
    peaks, totals = [], []
    for b in range(blocks):
        part = scores[b // per][b % per * BLOCK : (b % per + 1) * BLOCK]
        peak = jnp.max(part, axis=0, keepdims=True)
        totals.append(jnp.sum(jnp.exp2((part - peak) * (SCALE * LOG2E)), axis=0, keepdims=True))
        peaks.append(peak)
    group_peak = jnp.full((A, count), neg_floor, jnp.float32)
    for b in range(blocks):
        group_peak = jnp.where(members[b], jnp.maximum(group_peak, peaks[b]), group_peak)
    group_total = jnp.zeros((A, count), jnp.float32)
    for b in range(blocks):
        weight = totals[b] * jnp.exp2((peaks[b] - group_peak) * (SCALE * LOG2E))
        group_total = group_total + jnp.where(members[b], weight, 0.0)
    return jnp.where(group_total > 0, SCALE * group_peak + jnp.log(group_total), neg_floor)


def stage_body(
    refs_ref, queries_ref, labels_in, taps_in, bias_in, _,
    out_ref, mine_ref, members_ref, consts_ref,
    chunks, labels_ref, taps_ref, bias_ref, sems,
):
    count, step = chunks.shape[0], chunks.shape[1]
    copies = [
        pltpu.make_async_copy(refs_ref.at[pl.ds(c * step, step)], chunks.at[c], sems.at[c])
        for c in range(count)
    ]
    small = [(labels_in, labels_ref), (taps_in, taps_ref), (bias_in, bias_ref)]
    small.append((queries_ref, mine_ref))
    for source, target in small:
        copies.append(pltpu.make_async_copy(source, target, sems.at[len(copies)]))
    for copy in copies[count:] + copies[:count]:
        copy.start()
    for copy in copies[count:]:
        copy.wait()
    ancestry = lax.broadcasted_iota(jnp.int32, (A, BLOCK), 0)
    for b in range(members_ref.shape[0]):
        members_ref[b] = (ancestry == labels_ref[b]).astype(jnp.float32)
    same = lax.broadcasted_iota(jnp.int32, (A, A), 0) == lax.broadcasted_iota(jnp.int32, (A, A), 1)
    bias = jnp.sum(jnp.where(same, bias_ref[...], 0.0), axis=1, keepdims=True)
    for tap in range(TAPS):
        consts_ref[tap] = jnp.broadcast_to(taps_ref[:, tap : tap + 1], (A, BLOCK))
    consts_ref[TAPS] = jnp.broadcast_to(bias, (A, BLOCK))
    for c in range(count):
        copies[c].wait()
        out_ref[c * step : (c + 1) * step] = chunks[c].astype(narrow)


def stage(references, queries, labels, kernel, class_bias, block):
    step = 128
    count = references.shape[0] // step
    operands = (references, queries, labels, kernel.T, class_bias[None, :])
    return pl.pallas_call(
        stage_body,
        out_shape=(
            pltpu.VMEM(references.shape, narrow),
            pltpu.VMEM(queries.shape, queries.dtype),
            pltpu.VMEM((references.shape[0] // BLOCK, A, BLOCK), jnp.float32),
            pltpu.VMEM((TAPS + 1, A, BLOCK), jnp.float32),
        ),
        in_specs=[anywhere] * (len(operands) + 1),
        out_specs=(vmem,) * 4,
        scratch_shapes=[
            pltpu.VMEM((count, step, references.shape[1]), references.dtype),
            pltpu.SMEM(labels.shape, labels.dtype),
            pltpu.VMEM((A, TAPS), kernel.dtype),
            pltpu.VMEM((1, A), class_bias.dtype),
            pltpu.SemaphoreType.DMA((count + 4,)),
        ],
        cost_estimate=pl.CostEstimate(
            flops=references.size, bytes_accessed=3 * references.size, transcendentals=0
        ),
        compiler_params=pltpu.CompilerParams(vmem_limit_bytes=40 << 20),
        name="stage",
    )(
        *(pltpu.with_memory_space_constraint(x, pltpu.HBM) for x in operands),
        pltpu.with_memory_space_constraint(block, pltpu.VMEM),
    )


def pool_tiles(members_ref, refs_ref, query_refs):
    windows = refs_ref.shape[1] // S
    odd = lax.axis_index("win") % 2 == 1
    rows = query_refs[0][0].shape[0]
    count = rows * len(query_refs)
    members = [members_ref[b] > 0.5 for b in range(members_ref.shape[0])]
    if count != BLOCK:
        members = [
            jnp.broadcast_to(members_ref[b][:, :1], (A, count)) > 0.5 for b in range(len(members))
        ]
    pooled = []
    for window in range(windows):
        cols = slice(window * S, (window + 1) * S)
        queries = jnp.concatenate(
            [q[0][:, cols] if len(q) == 1 else jnp.where(odd, q[1][:, cols], q[0][:, cols]) for q in query_refs],
            axis=0,
        )
        queries = queries.astype(narrow)
        parts = refs_ref.shape[0] // PART
        scores = [
            lax.dot_general(
                refs_ref[part * PART : (part + 1) * PART, cols],
                queries,
                (((1,), (1,)), ((), ())),
                preferred_element_type=jnp.float32,
            )
            for part in range(parts)
        ]
        pooled.append(pool_window(scores, members))
    return [
        jnp.concatenate([p[:, j * rows : (j + 1) * rows] for p in pooled], axis=1)
        for j in range(len(query_refs))
    ]


def grouped(refs, sizes):
    refs = list(refs)
    return [[refs.pop(0) for _ in range(size)] for size in sizes]


def pool_body(sizes, members_ref, refs_ref, *rest):
    out_ref = rest[-1]
    for j, tile in enumerate(pool_tiles(members_ref, refs_ref, grouped(rest[:-1], sizes))):
        out_ref[j] = tile


def last_body(late, groups, sizes, members_ref, refs_ref, *rest):
    out_ref = rest[-1]
    here = lax.axis_index("ref")

    def place(offset, tile):
        for v in range(out_ref.shape[0]):
            out_ref[v, here ^ offset] = tile

    for ref, offsets in zip(rest[sum(sizes) : -1], groups, strict=True):
        for j, offset in enumerate(offsets):
            place(offset, ref[j])
    for offset, tile in zip(late, pool_tiles(members_ref, refs_ref, grouped(rest[: sum(sizes)], sizes)), strict=True):
        place(offset, tile)


def pool_cost(refs, queries):
    count = sum(q[0].shape[0] for q in queries)
    return pl.CostEstimate(
        flops=2 * refs.size * count,
        bytes_accessed=refs.size,
        transcendentals=refs.size // S * count,
    )


def pool(members, refs, queries):
    windows = refs.shape[1] // S
    rows = queries[0][0].shape[0]
    sizes = [len(q) for q in queries]
    return pl.pallas_call(
        functools.partial(pool_body, sizes),
        out_shape=pltpu.VMEM((len(queries), A, windows * rows), jnp.float32),
        in_specs=[vmem] * (2 + sum(sizes)),
        out_specs=vmem,
        cost_estimate=pool_cost(refs, queries),
        compiler_params=pltpu.CompilerParams(vmem_limit_bytes=40 << 20),
        name="pool",
    )(members, refs, *sum(map(list, queries), []))


def pool_last(members, refs, queries, late, tiles, groups, win, count):
    windows = refs.shape[1] // S
    rows = queries[0][0].shape[0]
    sizes = [len(q) for q in queries]
    return pl.pallas_call(
        functools.partial(last_body, late, groups, sizes),
        out_shape=pltpu.VMEM((win, count, A, windows * rows), jnp.float32),
        in_specs=[vmem] * (2 + sum(sizes) + len(tiles)),
        out_specs=vmem,
        cost_estimate=pool_cost(refs, queries),
        compiler_params=pltpu.CompilerParams(vmem_limit_bytes=40 << 20),
        name="pool_last",
    )(members, refs, *sum(map(list, queries), []), *tiles)


def finish_body(win, refs, windows, consts_ref, in_ref, out_ref):
    here = lax.axis_index("win")
    rows = out_ref.shape[2]

    def centered(block):
        parts = in_ref[pl.ds(block * refs, refs)]
        highest = jnp.max(parts, axis=0)
        pooled = highest + jnp.log(jnp.sum(jnp.exp(parts - highest[None]), axis=0))
        return pooled - jnp.mean(pooled, axis=0, keepdims=True)

    before = jnp.where(here > 0, centered(jnp.maximum(here - 1, 0)), 0.0)
    after = jnp.where(here < win - 1, centered(jnp.minimum(here + 1, win - 1)), 0.0)
    padded = jnp.concatenate([before, centered(here), after], axis=1)
    width = windows * rows
    total = jnp.zeros((A, width), jnp.float32)
    for tap in range(TAPS):
        start = width + (tap - HALF) * rows
        total = total + consts_ref[tap][:, :width] * padded[:, start : start + width]
    logits = total + consts_ref[TAPS][:, :width]
    shifted = logits - jnp.max(logits, axis=0, keepdims=True)
    result = shifted - jnp.log(jnp.sum(jnp.exp(shifted), axis=0, keepdims=True))
    for window in range(windows):
        out_ref[window] = result[:, window * rows : (window + 1) * rows]


def finish(received, consts, win, refs, windows, rows):
    return pl.pallas_call(
        functools.partial(finish_body, win, refs, windows),
        out_shape=jax.ShapeDtypeStruct((windows, A, rows), jnp.float32),
        in_specs=[vmem] * 2,
        out_specs=vmem,
        name="finish",
    )(*(pltpu.with_memory_space_constraint(x, pltpu.VMEM) for x in (consts, received)))


def exchange(block, offset, size):
    return lax.ppermute(block, "ref", [(i, i ^ offset) for i in range(size)])


def exchange_some(block, offset, size, core):
    wins = lax.axis_size("win")
    pairs = [
        (i * wins + w, (i ^ offset) * wins + w)
        for w in range(core, wins, 2)
        for i in range(size)
    ]
    return lax.ppermute(block, ("ref", "win"), pairs)


def gather_queries(queries, size):
    near = [k for k in range(4, size, 2) if k & 2]
    blocks = {}
    for k in near + [2, 1]:
        blocks[k] = exchange(queries, k, size)
    for k in near:
        blocks[k ^ 3] = (
            exchange_some(queries, k ^ 3, size, 0),
            exchange_some(blocks[1], k ^ 2, size, 1),
        )
    for k in near:
        blocks[k | 1] = exchange(blocks[k], 1, size)
    for k in near:
        blocks[k ^ 2] = exchange(blocks[k], 2, size)
    blocks[3] = exchange(blocks[2], 1, size)
    return blocks


def as_tuple(block):
    return block if isinstance(block, tuple) else (block,)


def per_device(queries, references, labels, kernel, class_bias):
    refs, win = lax.axis_size("ref"), lax.axis_size("win")
    windows = references.shape[1] // S
    rows = queries.shape[0]
    blocks = gather_queries(queries, refs)
    staged, mine, members, consts = stage(
        references, queries, labels, kernel, class_bias, blocks[2]
    )
    blocks[0] = mine
    first = [0, 1, 2, refs - 2]
    rest = [k for k in blocks if k not in first]
    cut = len(rest) - LAST
    groups = [first] + [rest[k : k + LAST] for k in range(0, cut, LAST)]
    late = rest[cut:]
    tiles = [pool(members, staged, [as_tuple(blocks[k]) for k in group]) for group in groups]
    sent = pool_last(members, staged, [as_tuple(blocks[k]) for k in late], late, tiles, groups, win, refs)
    sent = sent.reshape((win * refs,) + sent.shape[2:])
    received = lax.all_to_all(sent, ("win", "ref"), split_axis=0, concat_axis=0, tiled=True)
    return finish(received, consts, win, refs, windows, rows)


def solution(mesh):
    in_specs = (P("ref", "win"), P("ref", "win"), P("ref"), P(), P())
    out_specs = P("win", None, "ref")
    return jax.shard_map(
        per_device, mesh=mesh, in_specs=in_specs, out_specs=out_specs, check_vma=False
    )
```

```python
import functools

import jax
import jax.numpy as jnp
from jax import lax
from jax.experimental import pallas as pl
from jax.experimental.pallas import tpu as pltpu
from jax.sharding import PartitionSpec as P

S = 512
A = 8
BLOCK = 128
TAPS = 9
HALF = TAPS // 2
LAST = 4
PART = 256

LOG2E = 1.4426950408889634
SCALE = 256.0 / S

neg_floor = -1e30
narrow = jnp.float8_e4m3fn
vmem = pl.BlockSpec(memory_space=pltpu.VMEM)
anywhere = pl.BlockSpec(memory_space=pl.ANY)


def pool_window(scores, members):
    count = scores[0].shape[1]
    per = scores[0].shape[0] // BLOCK
    blocks = per * len(scores)
    peaks, totals = [], []
    for b in range(blocks):
        part = scores[b // per][b % per * BLOCK : (b % per + 1) * BLOCK]
        peak = jnp.max(part, axis=0, keepdims=True)
        totals.append(jnp.sum(jnp.exp2((part - peak) * (SCALE * LOG2E)), axis=0, keepdims=True))
        peaks.append(peak)
    group_peak = jnp.full((A, count), neg_floor, jnp.float32)
    for b in range(blocks):
        group_peak = jnp.where(members[b], jnp.maximum(group_peak, peaks[b]), group_peak)
    group_total = jnp.zeros((A, count), jnp.float32)
    for b in range(blocks):
        weight = totals[b] * jnp.exp2((peaks[b] - group_peak) * (SCALE * LOG2E))
        group_total = group_total + jnp.where(members[b], weight, 0.0)
    return jnp.where(group_total > 0, SCALE * group_peak + jnp.log(group_total), neg_floor)


def stage_body(
    refs_ref, queries_ref, labels_in, taps_in, bias_in, _,
    out_ref, mine_ref, members_ref, consts_ref,
    chunks, labels_ref, taps_ref, bias_ref, sems,
):
    count, step = chunks.shape[0], chunks.shape[1]
    copies = [
        pltpu.make_async_copy(refs_ref.at[pl.ds(c * step, step)], chunks.at[c], sems.at[c])
        for c in range(count)
    ]
    small = [(labels_in, labels_ref), (taps_in, taps_ref), (bias_in, bias_ref)]
    small.append((queries_ref, mine_ref))
    for source, target in small:
        copies.append(pltpu.make_async_copy(source, target, sems.at[len(copies)]))
    for copy in copies[count:] + copies[:count]:
        copy.start()
    for copy in copies[count:]:
        copy.wait()
    ancestry = lax.broadcasted_iota(jnp.int32, (A, BLOCK), 0)
    for b in range(members_ref.shape[0]):
        members_ref[b] = (ancestry == labels_ref[b]).astype(jnp.float32)
    same = lax.broadcasted_iota(jnp.int32, (A, A), 0) == lax.broadcasted_iota(jnp.int32, (A, A), 1)
    bias = jnp.sum(jnp.where(same, bias_ref[...], 0.0), axis=1, keepdims=True)
    for tap in range(TAPS):
        consts_ref[tap] = jnp.broadcast_to(taps_ref[:, tap : tap + 1], (A, BLOCK))
    consts_ref[TAPS] = jnp.broadcast_to(bias, (A, BLOCK))
    for c in range(count):
        copies[c].wait()
        out_ref[c * step : (c + 1) * step] = chunks[c].astype(narrow)


def stage(references, queries, labels, kernel, class_bias, block):
    step = 128
    count = references.shape[0] // step
    operands = (references, queries, labels, kernel.T, class_bias[None, :])
    return pl.pallas_call(
        stage_body,
        out_shape=(
            pltpu.VMEM(references.shape, narrow),
            pltpu.VMEM(queries.shape, queries.dtype),
            pltpu.VMEM((references.shape[0] // BLOCK, A, BLOCK), jnp.float32),
            pltpu.VMEM((TAPS + 1, A, BLOCK), jnp.float32),
        ),
        in_specs=[anywhere] * (len(operands) + 1),
        out_specs=(vmem,) * 4,
        scratch_shapes=[
            pltpu.VMEM((count, step, references.shape[1]), references.dtype),
            pltpu.SMEM(labels.shape, labels.dtype),
            pltpu.VMEM((A, TAPS), kernel.dtype),
            pltpu.VMEM((1, A), class_bias.dtype),
            pltpu.SemaphoreType.DMA((count + 4,)),
        ],
        cost_estimate=pl.CostEstimate(
            flops=references.size, bytes_accessed=3 * references.size, transcendentals=0
        ),
        compiler_params=pltpu.CompilerParams(vmem_limit_bytes=40 << 20),
        name="stage",
    )(
        *(pltpu.with_memory_space_constraint(x, pltpu.HBM) for x in operands),
        pltpu.with_memory_space_constraint(block, pltpu.VMEM),
    )


def pool_tiles(members_ref, refs_ref, query_refs):
    windows = refs_ref.shape[1] // S
    odd = lax.axis_index("win") % 2 == 1
    rows = query_refs[0][0].shape[0]
    count = rows * len(query_refs)
    members = [members_ref[b] > 0.5 for b in range(members_ref.shape[0])]
    if count != BLOCK:
        members = [
            jnp.broadcast_to(members_ref[b][:, :1], (A, count)) > 0.5 for b in range(len(members))
        ]
    pooled = []
    for window in range(windows):
        cols = slice(window * S, (window + 1) * S)
        queries = jnp.concatenate(
            [q[0][:, cols] if len(q) == 1 else jnp.where(odd, q[1][:, cols], q[0][:, cols]) for q in query_refs],
            axis=0,
        )
        queries = queries.astype(narrow)
        parts = refs_ref.shape[0] // PART
        scores = [
            lax.dot_general(
                refs_ref[part * PART : (part + 1) * PART, cols],
                queries,
                (((1,), (1,)), ((), ())),
                preferred_element_type=jnp.float32,
            )
            for part in range(parts)
        ]
        pooled.append(pool_window(scores, members))
    return [
        jnp.concatenate([p[:, j * rows : (j + 1) * rows] for p in pooled], axis=1)
        for j in range(len(query_refs))
    ]


def grouped(refs, sizes):
    refs = list(refs)
    return [[refs.pop(0) for _ in range(size)] for size in sizes]


def pool_body(sizes, members_ref, refs_ref, *rest):
    out_ref = rest[-1]
    for j, tile in enumerate(pool_tiles(members_ref, refs_ref, grouped(rest[:-1], sizes))):
        out_ref[j] = tile


def last_body(late, groups, sizes, members_ref, refs_ref, *rest):
    out_ref = rest[-1]
    here = lax.axis_index("ref")

    def place(offset, tile):
        for v in range(out_ref.shape[0]):
            out_ref[v, here ^ offset] = tile

    for ref, offsets in zip(rest[sum(sizes) : -1], groups, strict=True):
        for j, offset in enumerate(offsets):
            place(offset, ref[j])
    for offset, tile in zip(late, pool_tiles(members_ref, refs_ref, grouped(rest[: sum(sizes)], sizes)), strict=True):
        place(offset, tile)


def pool_cost(refs, queries):
    count = sum(q[0].shape[0] for q in queries)
    return pl.CostEstimate(
        flops=2 * refs.size * count,
        bytes_accessed=refs.size,
        transcendentals=refs.size // S * count,
    )


def pool(members, refs, queries):
    windows = refs.shape[1] // S
    rows = queries[0][0].shape[0]
    sizes = [len(q) for q in queries]
    return pl.pallas_call(
        functools.partial(pool_body, sizes),
        out_shape=pltpu.VMEM((len(queries), A, windows * rows), jnp.float32),
        in_specs=[vmem] * (2 + sum(sizes)),
        out_specs=vmem,
        cost_estimate=pool_cost(refs, queries),
        compiler_params=pltpu.CompilerParams(vmem_limit_bytes=40 << 20),
        name="pool",
    )(members, refs, *sum(map(list, queries), []))


def pool_last(members, refs, queries, late, tiles, groups, win, count):
    windows = refs.shape[1] // S
    rows = queries[0][0].shape[0]
    sizes = [len(q) for q in queries]
    return pl.pallas_call(
        functools.partial(last_body, late, groups, sizes),
        out_shape=pltpu.VMEM((win, count, A, windows * rows), jnp.float32),
        in_specs=[vmem] * (2 + sum(sizes) + len(tiles)),
        out_specs=vmem,
        cost_estimate=pool_cost(refs, queries),
        compiler_params=pltpu.CompilerParams(vmem_limit_bytes=40 << 20),
        name="pool_last",
    )(members, refs, *sum(map(list, queries), []), *tiles)


def finish_body(win, refs, windows, consts_ref, in_ref, out_ref):
    here = lax.axis_index("win")
    rows = out_ref.shape[2]

    def centered(block):
        parts = in_ref[pl.ds(block * refs, refs)]
        highest = jnp.max(parts, axis=0)
        pooled = highest + jnp.log(jnp.sum(jnp.exp(parts - highest[None]), axis=0))
        return pooled - jnp.mean(pooled, axis=0, keepdims=True)

    before = jnp.where(here > 0, centered(jnp.maximum(here - 1, 0)), 0.0)
    after = jnp.where(here < win - 1, centered(jnp.minimum(here + 1, win - 1)), 0.0)
    now = centered(here)
    width = windows * rows
    lane = lax.broadcasted_iota(jnp.int32, (A, width), 1)
    total = consts_ref[HALF][:, :width] * now
    for step in range(1, HALF + 1):
        moved = step * rows
        if moved == width:
            low, high = before, after
        else:
            low = pltpu.roll(jnp.where(lane < width - moved, now, before), moved, 1)
            high = pltpu.roll(jnp.where(lane >= moved, now, after), width - moved, 1)
        total = total + consts_ref[HALF - step][:, :width] * low
        total = total + consts_ref[HALF + step][:, :width] * high
    logits = total + consts_ref[TAPS][:, :width]
    shifted = logits - jnp.max(logits, axis=0, keepdims=True)
    result = shifted - jnp.log(jnp.sum(jnp.exp(shifted), axis=0, keepdims=True))
    for window in range(windows):
        out_ref[window] = result[:, window * rows : (window + 1) * rows]


def finish(received, consts, win, refs, windows, rows):
    return pl.pallas_call(
        functools.partial(finish_body, win, refs, windows),
        out_shape=jax.ShapeDtypeStruct((windows, A, rows), jnp.float32),
        in_specs=[vmem] * 2,
        out_specs=vmem,
        name="finish",
    )(*(pltpu.with_memory_space_constraint(x, pltpu.VMEM) for x in (consts, received)))


def exchange(block, offset, size):
    return lax.ppermute(block, "ref", [(i, i ^ offset) for i in range(size)])


def exchange_some(block, offset, size, core):
    wins = lax.axis_size("win")
    pairs = [
        (i * wins + w, (i ^ offset) * wins + w)
        for w in range(core, wins, 2)
        for i in range(size)
    ]
    return lax.ppermute(block, ("ref", "win"), pairs)


def gather_queries(queries, size):
    near = [k for k in range(4, size, 2) if k & 2]
    blocks = {}
    for k in near + [2, 1]:
        blocks[k] = exchange(queries, k, size)
    for k in near:
        blocks[k ^ 3] = (
            exchange_some(queries, k ^ 3, size, 0),
            exchange_some(blocks[1], k ^ 2, size, 1),
        )
    for k in near:
        blocks[k | 1] = exchange(blocks[k], 1, size)
    for k in near:
        blocks[k ^ 2] = exchange(blocks[k], 2, size)
    blocks[3] = exchange(blocks[2], 1, size)
    return blocks


def as_tuple(block):
    return block if isinstance(block, tuple) else (block,)


def per_device(queries, references, labels, kernel, class_bias):
    refs, win = lax.axis_size("ref"), lax.axis_size("win")
    windows = references.shape[1] // S
    rows = queries.shape[0]
    blocks = gather_queries(queries, refs)
    staged, mine, members, consts = stage(
        references, queries, labels, kernel, class_bias, blocks[2]
    )
    blocks[0] = mine
    first = [0, 1, 2, refs - 2]
    rest = [k for k in blocks if k not in first]
    cut = len(rest) - LAST
    groups = [first] + [rest[k : k + LAST] for k in range(0, cut, LAST)]
    late = rest[cut:]
    tiles = [pool(members, staged, [as_tuple(blocks[k]) for k in group]) for group in groups]
    sent = pool_last(members, staged, [as_tuple(blocks[k]) for k in late], late, tiles, groups, win, refs)
    sent = sent.reshape((win * refs,) + sent.shape[2:])
    received = lax.all_to_all(sent, ("win", "ref"), split_axis=0, concat_axis=0, tiled=True)
    return finish(received, consts, win, refs, windows, rows)


def solution(mesh):
    in_specs = (P("ref", "win"), P("ref", "win"), P("ref"), P(), P())
    out_specs = P("win", None, "ref")
    return jax.shard_map(
        per_device, mesh=mesh, in_specs=in_specs, out_specs=out_specs, check_vma=False
    )
```

```python
import functools

import jax
import jax.numpy as jnp
from jax import lax
from jax.experimental import pallas as pl
from jax.experimental.pallas import tpu as pltpu
from jax.sharding import PartitionSpec as P

S = 512
A = 8
BLOCK = 128
TAPS = 9
HALF = TAPS // 2
LAST = 4
PART = 256

LOG2E = 1.4426950408889634
SCALE = 256.0 / S

neg_floor = -1e30
narrow = jnp.float8_e4m3fn
vmem = pl.BlockSpec(memory_space=pltpu.VMEM)
anywhere = pl.BlockSpec(memory_space=pl.ANY)


def pool_window(scores, members):
    count = scores[0].shape[1]
    per = scores[0].shape[0] // BLOCK
    blocks = per * len(scores)
    peaks, totals = [], []
    for b in range(blocks):
        part = scores[b // per][b % per * BLOCK : (b % per + 1) * BLOCK]
        peak = jnp.max(part, axis=0, keepdims=True)
        totals.append(jnp.sum(jnp.exp2((part - peak) * (SCALE * LOG2E)), axis=0, keepdims=True))
        peaks.append(peak)
    group_peak = jnp.full((A, count), neg_floor, jnp.float32)
    for b in range(blocks):
        group_peak = jnp.where(members[b], jnp.maximum(group_peak, peaks[b]), group_peak)
    group_total = jnp.zeros((A, count), jnp.float32)
    for b in range(blocks):
        weight = totals[b] * jnp.exp2((peaks[b] - group_peak) * (SCALE * LOG2E))
        group_total = group_total + jnp.where(members[b], weight, 0.0)
    return jnp.where(group_total > 0, SCALE * group_peak + jnp.log(group_total), neg_floor)


def stage_body(
    refs_ref, queries_ref, labels_in, taps_in, bias_in, _,
    out_ref, mine_ref, members_ref, consts_ref,
    chunks, labels_ref, taps_ref, bias_ref, sems,
):
    count, step = chunks.shape[0], chunks.shape[1]
    copies = [
        pltpu.make_async_copy(refs_ref.at[pl.ds(c * step, step)], chunks.at[c], sems.at[c])
        for c in range(count)
    ]
    small = [(labels_in, labels_ref), (taps_in, taps_ref), (bias_in, bias_ref)]
    small.append((queries_ref, mine_ref))
    for source, target in small:
        copies.append(pltpu.make_async_copy(source, target, sems.at[len(copies)]))
    for copy in copies[count:] + copies[:count]:
        copy.start()
    for copy in copies[count:]:
        copy.wait()
    ancestry = lax.broadcasted_iota(jnp.int32, (A, BLOCK), 0)
    for b in range(members_ref.shape[0]):
        members_ref[b] = (ancestry == labels_ref[b]).astype(jnp.float32)
    same = lax.broadcasted_iota(jnp.int32, (A, A), 0) == lax.broadcasted_iota(jnp.int32, (A, A), 1)
    bias = jnp.sum(jnp.where(same, bias_ref[...], 0.0), axis=1, keepdims=True)
    for tap in range(TAPS):
        consts_ref[tap] = jnp.broadcast_to(taps_ref[:, tap : tap + 1], (A, BLOCK))
    consts_ref[TAPS] = jnp.broadcast_to(bias, (A, BLOCK))
    for c in range(count):
        copies[c].wait()
        out_ref[c * step : (c + 1) * step] = chunks[c].astype(narrow)


def stage(references, queries, labels, kernel, class_bias, block):
    step = 128
    count = references.shape[0] // step
    operands = (references, queries, labels, kernel.T, class_bias[None, :])
    return pl.pallas_call(
        stage_body,
        out_shape=(
            pltpu.VMEM(references.shape, narrow),
            pltpu.VMEM(queries.shape, queries.dtype),
            pltpu.VMEM((references.shape[0] // BLOCK, A, BLOCK), jnp.float32),
            pltpu.VMEM((TAPS + 1, A, BLOCK), jnp.float32),
        ),
        in_specs=[anywhere] * (len(operands) + 1),
        out_specs=(vmem,) * 4,
        scratch_shapes=[
            pltpu.VMEM((count, step, references.shape[1]), references.dtype),
            pltpu.SMEM(labels.shape, labels.dtype),
            pltpu.VMEM((A, TAPS), kernel.dtype),
            pltpu.VMEM((1, A), class_bias.dtype),
            pltpu.SemaphoreType.DMA((count + 4,)),
        ],
        cost_estimate=pl.CostEstimate(
            flops=references.size, bytes_accessed=3 * references.size, transcendentals=0
        ),
        compiler_params=pltpu.CompilerParams(vmem_limit_bytes=40 << 20),
        name="stage",
    )(
        *(pltpu.with_memory_space_constraint(x, pltpu.HBM) for x in operands),
        pltpu.with_memory_space_constraint(block, pltpu.VMEM),
    )


def pool_tiles(members_ref, refs_ref, query_refs):
    windows = refs_ref.shape[1] // S
    odd = lax.axis_index("win") % 2 == 1
    rows = query_refs[0][0].shape[0]
    count = rows * len(query_refs)
    members = [members_ref[b] > 0.5 for b in range(members_ref.shape[0])]
    if count != BLOCK:
        members = [
            jnp.broadcast_to(members_ref[b][:, :1], (A, count)) > 0.5 for b in range(len(members))
        ]
    pooled = []
    for window in range(windows):
        cols = slice(window * S, (window + 1) * S)
        queries = jnp.concatenate(
            [q[0][:, cols] if len(q) == 1 else jnp.where(odd, q[1][:, cols], q[0][:, cols]) for q in query_refs],
            axis=0,
        )
        queries = queries.astype(narrow)
        parts = refs_ref.shape[0] // PART
        scores = [
            lax.dot_general(
                refs_ref[part * PART : (part + 1) * PART, cols],
                queries,
                (((1,), (1,)), ((), ())),
                preferred_element_type=jnp.float32,
            )
            for part in range(parts)
        ]
        pooled.append(pool_window(scores, members))
    return [
        jnp.concatenate([p[:, j * rows : (j + 1) * rows] for p in pooled], axis=1)
        for j in range(len(query_refs))
    ]


def grouped(refs, sizes):
    refs = list(refs)
    return [[refs.pop(0) for _ in range(size)] for size in sizes]


def pool_body(sizes, members_ref, refs_ref, *rest):
    out_ref = rest[-1]
    for j, tile in enumerate(pool_tiles(members_ref, refs_ref, grouped(rest[:-1], sizes))):
        out_ref[j] = tile


def last_body(late, groups, sizes, members_ref, refs_ref, *rest):
    out_ref = rest[-1]
    here = lax.axis_index("ref")

    def place(offset, tile):
        for v in range(out_ref.shape[0]):
            out_ref[v, here ^ offset] = tile

    for ref, offsets in zip(rest[sum(sizes) : -1], groups, strict=True):
        for j, offset in enumerate(offsets):
            place(offset, ref[j])
    for offset, tile in zip(late, pool_tiles(members_ref, refs_ref, grouped(rest[: sum(sizes)], sizes)), strict=True):
        place(offset, tile)


def pool_cost(refs, queries):
    count = sum(q[0].shape[0] for q in queries)
    return pl.CostEstimate(
        flops=2 * refs.size * count,
        bytes_accessed=refs.size,
        transcendentals=refs.size // S * count,
    )


def pool(members, refs, queries):
    windows = refs.shape[1] // S
    rows = queries[0][0].shape[0]
    sizes = [len(q) for q in queries]
    return pl.pallas_call(
        functools.partial(pool_body, sizes),
        out_shape=pltpu.VMEM((len(queries), A, windows * rows), jnp.float32),
        in_specs=[vmem] * (2 + sum(sizes)),
        out_specs=vmem,
        cost_estimate=pool_cost(refs, queries),
        compiler_params=pltpu.CompilerParams(vmem_limit_bytes=40 << 20),
        name="pool",
    )(members, refs, *sum(map(list, queries), []))


def pool_last(members, refs, queries, late, tiles, groups, win, count):
    windows = refs.shape[1] // S
    rows = queries[0][0].shape[0]
    sizes = [len(q) for q in queries]
    return pl.pallas_call(
        functools.partial(last_body, late, groups, sizes),
        out_shape=pltpu.VMEM((win, count, A, windows * rows), jnp.float32),
        in_specs=[vmem] * (2 + sum(sizes) + len(tiles)),
        out_specs=vmem,
        cost_estimate=pool_cost(refs, queries),
        compiler_params=pltpu.CompilerParams(vmem_limit_bytes=40 << 20),
        name="pool_last",
    )(members, refs, *sum(map(list, queries), []), *tiles)


def finish_body(win, refs, windows, consts_ref, in_ref, out_ref):
    here = lax.axis_index("win")
    rows = out_ref.shape[2]

    def centered(block):
        parts = in_ref[pl.ds(block * refs, refs)]
        highest = jnp.max(parts, axis=0)
        pooled = highest + jnp.log(jnp.sum(jnp.exp(parts - highest[None]), axis=0))
        return pooled - jnp.mean(pooled, axis=0, keepdims=True)

    before = jnp.where(here > 0, centered(jnp.maximum(here - 1, 0)), 0.0)
    after = jnp.where(here < win - 1, centered(jnp.minimum(here + 1, win - 1)), 0.0)
    now = centered(here)
    width = windows * rows
    lane = lax.broadcasted_iota(jnp.int32, (A, width), 1)
    total = consts_ref[HALF][:, :width] * now
    for step in range(1, HALF + 1):
        moved = step * rows
        if moved == width:
            low, high = before, after
        else:
            low = pltpu.roll(jnp.where(lane < width - moved, now, before), moved, 1)
            high = pltpu.roll(jnp.where(lane >= moved, now, after), width - moved, 1)
        total = total + consts_ref[HALF - step][:, :width] * low
        total = total + consts_ref[HALF + step][:, :width] * high
    logits = total + consts_ref[TAPS][:, :width]
    shifted = logits - jnp.max(logits, axis=0, keepdims=True)
    result = shifted - jnp.log(jnp.sum(jnp.exp(shifted), axis=0, keepdims=True))
    for window in range(windows):
        out_ref[window] = result[:, window * rows : (window + 1) * rows]


def finish(received, consts, win, refs, windows, rows):
    return pl.pallas_call(
        functools.partial(finish_body, win, refs, windows),
        out_shape=jax.ShapeDtypeStruct((windows, A, rows), jnp.float32),
        in_specs=[vmem] * 2,
        out_specs=vmem,
        name="finish",
    )(*(pltpu.with_memory_space_constraint(x, pltpu.VMEM) for x in (consts, received)))


def exchange(block, offset, size):
    return lax.ppermute(block, "ref", [(i, i ^ offset) for i in range(size)])


def exchange_some(block, offset, size, core):
    wins = lax.axis_size("win")
    pairs = [
        (i * wins + w, (i ^ offset) * wins + w)
        for w in range(core, wins, 2)
        for i in range(size)
    ]
    return lax.ppermute(block, ("ref", "win"), pairs)


def gather_queries(queries, size):
    near = [k for k in range(4, size, 2) if k & 2]
    blocks = {}
    for k in near + [2, 1]:
        blocks[k] = exchange(queries, k, size)
    for k in near:
        blocks[k ^ 3] = (
            exchange_some(queries, k ^ 3, size, 0),
            exchange_some(blocks[1], k ^ 2, size, 1),
        )
    for k in near:
        blocks[k | 1] = exchange(blocks[k], 1, size)
    for k in near:
        blocks[k ^ 2] = exchange(blocks[k], 2, size)
    blocks[3] = exchange(blocks[2], 1, size)
    return blocks


def as_tuple(block):
    return block if isinstance(block, tuple) else (block,)


def per_device(queries, references, labels, kernel, class_bias):
    refs, win = lax.axis_size("ref"), lax.axis_size("win")
    windows = references.shape[1] // S
    rows = queries.shape[0]
    blocks = gather_queries(queries, refs)
    staged, mine, members, consts = stage(
        references, queries, labels, kernel, class_bias, blocks[2]
    )
    blocks[0] = mine
    first = [1, 0, 2, refs - 2]
    rest = [k for k in blocks if k not in first]
    cut = len(rest) - LAST
    groups = [first] + [rest[k : k + LAST] for k in range(0, cut, LAST)]
    late = rest[cut:]
    tiles = [pool(members, staged, [as_tuple(blocks[k]) for k in group]) for group in groups]
    sent = pool_last(members, staged, [as_tuple(blocks[k]) for k in late], late, tiles, groups, win, refs)
    sent = sent.reshape((win * refs,) + sent.shape[2:])
    received = lax.all_to_all(sent, ("win", "ref"), split_axis=0, concat_axis=0, tiled=True)
    return finish(received, consts, win, refs, windows, rows)


def solution(mesh):
    in_specs = (P("ref", "win"), P("ref", "win"), P("ref"), P(), P())
    out_specs = P("win", None, "ref")
    return jax.shard_map(
        per_device, mesh=mesh, in_specs=in_specs, out_specs=out_specs, check_vma=False
    )
```
